512 devices in a mesh: strip: 16 (over z, core), date: 32 (over x, y).
Axes of the slice: x: 4, y: 8, z: 8, core: 2. Of those that a mesh axis runs over, the one named last changes fastest.
Arguments:
- images: bfloat16 [512, 1024, 128], P('date', 'strip'), may hold values from 0.19921875 to 5
- inverse_blocks: float32 [2, 32, 512, 512], P(None, 'strip', 'date'), as said below
- pair_first: int32 [1024], P('date'), may hold values from 0 to 15
- pair_block: int32 [1024, 1], P('date'), may hold values from 0 to 31; in each aligned block of 32 rows (0 to 31, 32 to 63, ...) at most 2 rows name the same one
- pair_second: int32 [1024], P('date'), may hold values from 0 to 15
- pair_count: int32 [32], P('date'), may hold values from 8 to 32, as said below
- shifts: int32 [1024, 2, 32], P('date', None, 'strip'), may hold values from -8 to 8
- anchors: int32 [32], P('strip'), may hold values from 0 to 96, as said below
Outputs:
- pair_offsets: float32 [1024, 2, 32], P('date', None, 'strip')
- series: float32 [2, 32, 512], P(None, 'strip', 'date')
The draws below stay inside these ranges and needn't reach their ends.
Inputs may be any that keep to these rules, and one draw needn't show every extreme that they name: `pair_block`: among the 32 slots of one date block at most 2 name one partner block, and some block is named that often. `pair_count`: slots 0 to count - 1 of a date block are live; slots at or past the count carry no pair, and their partner windows need not be sent. One block has all 32 live, one has 8, every other block 24 or more. `anchors`: chip q starts at column (q % 2) * 64 plus 0 to 32. `inverse_blocks`: symmetric in its last two dimensions.
All inputs are finite; a program needn't handle non-finite values.
Results may differ from the reference program's by a relative error of at most 0.008.
Values may be sent and summed in bfloat16 or wider, within the bound.
No kernel may reach another device: no remote copies, remote signals or barrier semaphores. Data moves between devices by JAX's collectives and lax.ppermute only.
A program may use at most 64 MiB of HBM per device.

```python
import math
import jax
import jax.numpy as jnp
import numpy as np
from jax import lax

CHIP = 64
SMAX = 8
DATE_DEV = 16
NCHIP = 2
PAIR_DEV = 32
CAP = 2
BLOCKS = 32
NDATE = 512
PAIRS = 1024
COLS = 128
BAND_ROWS = 1024
CHIPS_ALL = 32


def draw_inverse_blocks(key, part):
    subkeys = jax.random.split(key, 2)
    noise_part = jax.random.normal(subkeys[0], (2, CHIPS_ALL, NDATE, NDATE), jnp.float32) * (0.5 / math.sqrt(NDATE))
    mirror = (noise_part + jnp.swapaxes(noise_part, 2, 3)) * (1.0 / math.sqrt(2.0))
    diag_vals = jnp.exp(jax.random.uniform(subkeys[1], (2, CHIPS_ALL, NDATE), jnp.float32, math.log(0.5), math.log(2.0)))
    result = mirror + diag_vals[..., None] * jnp.eye(NDATE, dtype=jnp.float32)
    return result


def draw_pair_count(key, part):
    subkeys = jax.random.split(key, 2)
    counts = jax.random.randint(subkeys[0], (BLOCKS,), 3 * PAIR_DEV // 4, PAIR_DEV + 1, jnp.int32)
    shuffled = jax.random.permutation(subkeys[1], BLOCKS)
    counts = counts.at[shuffled[0]].set(PAIR_DEV)
    counts = counts.at[shuffled[1]].set(PAIR_DEV // 4)
    return counts


def draw_anchors(key, part):
    chip_ids = jnp.arange(CHIPS_ALL, dtype=jnp.int32)
    offsets_in = jax.random.randint(key, (CHIPS_ALL,), 0, CHIP // 2 + 1, jnp.int32)
    offsets_in = offsets_in.at[0].set(0)
    offsets_in = offsets_in.at[CHIPS_ALL - 1].set(CHIP // 2)
    return chip_ids % NCHIP * CHIP + offsets_in


def touch_ends(entries, rng, least, largest):
    extent = entries.shape
    place = [jax.random.randint(jax.random.fold_in(rng, axis), (), 0, extent[axis]) for axis in range(len(extent))]
    entries = entries.at[tuple(place)].set(least)
    longest = extent.index(max(extent))
    place[longest] = (place[longest] + 1) % extent[longest]
    return entries.at[tuple(place)].set(largest)


def shard_levels(own_key, shape, pieces, low, top_value):
    loudness, own = 1.0, jax.random.fold_in(own_key, 6)
    for axis_at, shards_of in pieces:
        heights = jnp.exp(jax.random.uniform(jax.random.fold_in(own, axis_at), (shards_of,), jnp.float32, low / len(pieces), top_value / len(pieces)))
        loudness = loudness * jnp.repeat(heights, shape[axis_at] // shards_of).reshape([-1 if axis == axis_at else 1 for axis in range(len(shape))])
    return loudness


def routed_block(stream_key, own, number, rows, amount, top, limit, lean):
    sequence = jax.random.permutation(stream_key, amount)
    packed, usual = shares(amount, rows * top, limit, lean, True), shares(amount, rows * top, limit, lean, False)
    places = jnp.arange(amount)

    def named(tallies, turn):
        used = int((tallies > 0).sum())
        fixed = max(1, used // 4)
        moved = fixed + (places - fixed + turn * (used - fixed)) % max(1, amount - fixed)
        return jnp.zeros((amount,), jnp.int32).at[sequence[jnp.where(places < fixed, places, moved)]].set(jnp.asarray(tallies, jnp.int32))

    tallies = jnp.where(number % 4 == 0, named(packed, number // 4), named(usual, number - number // 4 - 1))
    mixed = jax.random.permutation(jax.random.fold_in(own, 3), amount)
    giver, sink = mixed[0:amount // 2 * 2:2], mixed[1:amount // 2 * 2:2]
    room = jnp.minimum(tallies[giver] - 1, limit - tallies[sink]) // 2
    room = jnp.where((giver == sequence[0]) | (sink == sequence[0]) | (tallies[sink] == 0), 0, jnp.maximum(room, 0))
    moved = jax.random.randint(jax.random.fold_in(own, 4), (amount // 2,), 0, 1 << 20) % (room + 1)
    tallies = tallies.at[giver].add(-moved).at[sink].add(moved)
    items = jnp.searchsorted(jnp.cumsum(tallies), jnp.arange(rows * top), side="right").astype(jnp.int32)
    grid = items.reshape(top, rows).T
    grid = grid[jax.random.permutation(jax.random.fold_in(own, 1), rows)]
    turn = jax.random.randint(jax.random.fold_in(own, 2), (rows, 1), 0, top)
    return jnp.take_along_axis(grid, (jnp.arange(top)[None, :] + turn) % top, axis=1)


def shares(count, total, limit, lean, full):
    portions = [(1 << 20) // math.isqrt(grade ** lean) + 1 for grade in range(1, count + 1)]
    largest = limit if full else min(limit, max(-(-total // count), total * portions[0] // sum(portions)))
    least = 1 if total - largest >= count - 1 else 0
    given, rest = [largest] + [least] * (count - 1), total - largest - least * (count - 1)
    while rest > 0:
        free = [i for i in range(1, count) if given[i] < largest] or [i for i in range(1, count) if given[i] < limit]
        pool, left = sum([portions[i] for i in free]), rest
        for i in free:
            extra = min(limit - given[i], max(1, left * portions[i] // pool), rest)
            given[i] = given[i] + extra
            rest = rest - extra
    return np.array(given)


def setup_inputs(seed: int = 0) -> dict:
    streams_of = jax.random.split(jax.random.key(seed), 9)
    images = jnp.clip(jnp.exp(math.log(5.0) - 3.2227897 * jax.random.uniform(streams_of[0], (NDATE, BAND_ROWS, COLS), jnp.float32) ** shard_levels(streams_of[0], (NDATE, BAND_ROWS, COLS), ((0, 32), (1, 16)), -0.2, 0.2)), 0.19921875, 5.0).astype(jnp.bfloat16)
    inverse_blocks = draw_inverse_blocks(jax.random.fold_in(streams_of[8], 71), 0)
    pair_first = touch_ends(jax.random.randint(streams_of[2], (PAIRS,), 0, DATE_DEV), jax.random.fold_in(streams_of[2], 1), 0, DATE_DEV - 1).astype(jnp.int32)
    pair_block_keys = jax.random.split(jax.random.fold_in(streams_of[3], 1), PAIRS // PAIR_DEV)
    pair_block_turns = jax.random.permutation(jax.random.fold_in(streams_of[3], 3), PAIRS // PAIR_DEV)
    pair_block = jax.vmap(lambda own, number: routed_block(jax.random.fold_in(streams_of[3], 2), own, number, PAIR_DEV, BLOCKS, 1, CAP, 1))(pair_block_keys, pair_block_turns).reshape((PAIRS, 1))
    pair_second = touch_ends(jax.random.randint(streams_of[4], (PAIRS,), 0, DATE_DEV), jax.random.fold_in(streams_of[4], 1), 0, DATE_DEV - 1).astype(jnp.int32)
    pair_count = draw_pair_count(jax.random.fold_in(streams_of[8], 71), 0)
    shifts = touch_ends(jax.random.randint(streams_of[6], (PAIRS, 2, CHIPS_ALL), -SMAX, SMAX + 1), jax.random.fold_in(streams_of[6], 1), -SMAX, SMAX).astype(jnp.int32)
    anchors = draw_anchors(jax.random.fold_in(streams_of[8], 71), 0)
    return {"images": images, "inverse_blocks": inverse_blocks, "pair_first": pair_first, "pair_block": pair_block, "pair_second": pair_second, "pair_count": pair_count, "shifts": shifts, "anchors": anchors}


def make_tables(length):
    counter = jnp.arange(length, dtype=jnp.int32)
    products = (counter[:, None] * counter[None, :]) % length
    radians = products.astype(jnp.float32) * (2.0 * math.pi / length)
    cosine = jnp.cos(radians)
    sine_part = -jnp.sin(radians)
    forward = jnp.concatenate([cosine, sine_part], axis=1).astype(jnp.bfloat16)
    over_len = 2 * length
    signed = jnp.where(counter < length // 2, counter, counter - length)
    places = jnp.arange(over_len, dtype=jnp.int32)
    turned = (signed[:, None] * places[None, :]) % over_len
    angles = turned.astype(jnp.float32) * (2.0 * math.pi / over_len)
    vcosine = jnp.cos(angles)
    vsine = jnp.sin(angles)
    top_rows = jnp.concatenate([vcosine, vsine], axis=1)
    low_rows = jnp.concatenate([-vsine, vcosine], axis=1)
    inverse_rows = jnp.concatenate([top_rows, low_rows], axis=0).astype(jnp.bfloat16)
    displace = (((places + length) % over_len) - length).astype(jnp.float32) * 0.5
    return (forward, cosine.astype(jnp.bfloat16), sine_part.astype(jnp.bfloat16), inverse_rows,
            vcosine.T.astype(jnp.bfloat16), vsine.T.astype(jnp.bfloat16), displace)


def product(form, left, right):
    return jnp.einsum(form, left.astype(jnp.float32), right.astype(jnp.float32), precision=lax.Precision.HIGHEST)


def spectra(windows, tables):
    forward, cosine_b, sine_b = tables[0], tables[1], tables[2]
    length = windows.shape[-1]
    values = windows.astype(jnp.float32)
    centred = (values - jnp.mean(values, axis=(1, 2), keepdims=True)).astype(jnp.bfloat16)
    section_one = product("bmn,nk->bmk", centred, forward).astype(jnp.bfloat16)
    with_cos = product("km,bmj->bkj", cosine_b, section_one)
    with_sin = product("km,bmj->bkj", sine_b, section_one)
    real_part = with_cos[:, :, :length] - with_sin[:, :, length:]
    imag_part = with_sin[:, :, :length] + with_cos[:, :, length:]
    return jnp.concatenate([real_part, imag_part], axis=2).astype(jnp.bfloat16)


def centroid(near_spec, far_spec, tables):
    inverse_rows, back_cos, back_sin, displace = tables[3], tables[4], tables[5], tables[6]
    length = near_spec.shape[-1] // 2
    near_re = near_spec[:, :, :length].astype(jnp.float32)
    near_im = near_spec[:, :, length:].astype(jnp.float32)
    far_re = far_spec[:, :, :length].astype(jnp.float32)
    far_im = far_spec[:, :, length:].astype(jnp.float32)
    cross_re = near_re * far_re + near_im * far_im
    cross_im = near_im * far_re - near_re * far_im
    cross_spec = jnp.concatenate([cross_re, cross_im], axis=2).astype(jnp.bfloat16)
    along = product("bun,nl->bul", cross_spec, inverse_rows).astype(jnp.bfloat16)
    half_width = along.shape[-1] // 2
    surface = product("ku,bul->bkl", back_cos, along[:, :, :half_width]) - product("ku,bul->bkl", back_sin, along[:, :, half_width:])
    energy = surface * surface
    norm_val = jnp.mean(energy, axis=(1, 2)) + 1e-6
    row_shift = jnp.mean(energy * displace[None, :, None], axis=(1, 2)) / norm_val
    col_shift = jnp.mean(energy * displace[None, None, :], axis=(1, 2)) / norm_val
    return jnp.stack([row_shift, col_shift], axis=1)


def reference(images, inverse_blocks, pair_first, pair_block, pair_second, pair_count, shifts, anchors):
    length = CHIP
    margin = SMAX
    tables = make_tables(length)
    padded = jnp.pad(images, ((0, 0), (margin, margin), (margin, margin + length // 2)))
    chip_ids = jnp.arange(CHIPS_ALL, dtype=jnp.int32)
    row_base = ((chip_ids // NCHIP) * length + margin).astype(jnp.int32)
    col_base = (anchors + margin).astype(jnp.int32)

    def cut_window(image_rows, row_at, col_at):
        return lax.dynamic_slice(image_rows, (row_at, col_at), (length, length))

    def one_pair(slot):
        block_id = slot // PAIR_DEV
        first_id = (block_id * DATE_DEV + pair_first[slot]).astype(jnp.int32)
        second_id = (pair_block[slot, 0] * DATE_DEV + pair_second[slot]).astype(jnp.int32)
        live_mask = ((slot % PAIR_DEV) < pair_count[block_id]).astype(jnp.float32)
        near_img = lax.dynamic_index_in_dim(padded, first_id, 0, keepdims=False)
        far_img = lax.dynamic_index_in_dim(padded, second_id, 0, keepdims=False)
        near_win = jax.vmap(cut_window, in_axes=(None, 0, 0))(near_img, row_base, col_base)
        far_win = jax.vmap(cut_window, in_axes=(None, 0, 0))(far_img, (row_base + shifts[slot, 0]).astype(jnp.int32), (col_base + shifts[slot, 1]).astype(jnp.int32))
        found = centroid(spectra(near_win, tables), spectra(far_win, tables), tables)
        return (shifts[slot].astype(jnp.float32) + found.T) * live_mask

    pair_offsets = lax.map(one_pair, jnp.arange(PAIRS, dtype=jnp.int32))
    slot_ids = jnp.arange(PAIRS, dtype=jnp.int32)
    first_all = ((slot_ids // PAIR_DEV) * DATE_DEV + pair_first).astype(jnp.int32)
    second_all = (pair_block[:, 0] * DATE_DEV + pair_second).astype(jnp.int32)
    rhs_all = jax.ops.segment_sum(pair_offsets, second_all, num_segments=NDATE) - jax.ops.segment_sum(pair_offsets, first_all, num_segments=NDATE)
    rhs_all = jnp.transpose(rhs_all, (1, 2, 0))
    series = jnp.einsum("xqde,xqe->xqd", inverse_blocks, rhs_all, precision=lax.Precision.HIGHEST)
    return (pair_offsets, series)
```

```python
import math

import jax
import jax.numpy as jnp
import ml_dtypes
import numpy as np
from jax import lax
from jax.experimental import pallas as pl
from jax.experimental.pallas import tpu as pltpu
from jax.sharding import PartitionSpec as P

SMAX = 8
CHIP = 64
LANES = 128
BATCH = 4
HIGH = lax.Precision.HIGHEST
F32 = jnp.float32
BF16 = jnp.bfloat16


def make_tables():
    counter = np.arange(CHIP)
    turn = 2.0 * math.pi * (counter[:, None] * counter[None, :] % CHIP) / CHIP
    cosine, sine = np.cos(turn), -np.sin(turn)
    zero = np.zeros((CHIP, CHIP))
    two = np.eye(2)
    columns = np.concatenate([np.kron(two, cosine), np.kron(two, sine)], axis=1)
    rows = np.block([[cosine, -sine], [sine, cosine]])
    over = 2 * CHIP
    places = np.arange(over)
    displace = ((places + CHIP) % over - CHIP) * 0.5
    odd = np.where(places == CHIP, 0.0, displace)
    signed = np.where(counter < CHIP // 2, counter, counter - CHIP)
    basis = np.exp(2j * math.pi * signed[:, None] * places[None, :] / over)
    basis[CHIP // 2] = np.cos(math.pi * places / 2)
    form = np.imag((basis.conj() * odd) @ basis.T) / over
    ends = -0.25 * np.outer((-1.0) ** counter, (-1.0) ** counter)
    left = np.block([[ends, -2.0 * form], [zero, ends]])
    ends2, form2 = np.kron(two, ends), np.kron(two, -2.0 * form.T)
    right = np.block([[ends2, np.zeros((LANES, LANES))], [form2, ends2]])
    return tuple(a.astype(ml_dtypes.bfloat16) for a in (columns, rows, left, right))


def dot(a, b, precision=None):
    return lax.dot_general(
        a, b, (((1,), (0,)), ((), ())), precision=precision, preferred_element_type=F32
    )


def dot_nt(a, b, precision=None):
    return lax.dot_general(
        a, b, (((1,), (1,)), ((), ())), precision=precision, preferred_element_type=F32
    )


def same_chip():
    row = lax.broadcasted_iota(jnp.int32, (LANES, LANES), 0)
    lane = lax.broadcasted_iota(jnp.int32, (LANES, LANES), 1)
    return ((row < CHIP) == (lane < CHIP)).astype(F32)


def pack_kernel(
    first_ref, block_ref, second_ref, count_ref, shifts_ref, anchors_ref, images_ref,
    send_ref, cut_ref, near_ref, facts_ref, tally_ref,
):
    dates = images_ref.shape[0]
    blocks = send_ref.shape[0]
    row = lax.broadcasted_iota(jnp.int32, (LANES, LANES), 0)
    lane = lax.broadcasted_iota(jnp.int32, (LANES, LANES), 1)
    column = lane + jnp.where(lane < CHIP, anchors_ref[0], anchors_ref[1] - CHIP)
    pick = (row == column).astype(F32).astype(BF16)
    sums = []
    for date in range(dates):
        window = dot(images_ref[date], pick)
        cut_ref[date] = window
        sums.append(jnp.sum(window, axis=0, keepdims=True))
    means = dot(jnp.concatenate(sums, axis=0), same_chip(), HIGH) * (1.0 / (CHIP * CHIP))
    for date in range(dates):
        near_ref[date] = (cut_ref[date] - means[date : date + 1]).astype(BF16)
    facts_ref[...] = jnp.zeros(facts_ref.shape, F32)
    for block in range(blocks):
        tally_ref[block] = 0
    place = lax.broadcasted_iota(jnp.int32, (1, LANES), 1)

    def one_slot(slot, carry):
        block = block_ref[slot, 0]
        rank = tally_ref[block]
        tally_ref[block] = rank + 1
        first = first_ref[slot]
        at = pl.multiple_of(rank * CHIP, CHIP)
        send_ref[block, pl.ds(at, CHIP), :] = near_ref[first]
        fact = jnp.where(place == 0, 1, 0)
        for index, value in enumerate(
            (
                second_ref[slot], first, shifts_ref[slot, 0, 0], shifts_ref[slot, 1, 0],
                shifts_ref[slot, 0, 1], shifts_ref[slot, 1, 1],
            )
        ):
            fact = jnp.where(place == index + 1, value, fact)
        facts_ref[pl.ds(block * 8 + rank, 1), :] = fact.astype(F32)
        return carry

    lax.fori_loop(0, count_ref[0], one_slot, 0)
    send_ref[:, 2 * CHIP : 2 * CHIP + 8, :] = (
        facts_ref[...].reshape(blocks, 8, LANES).astype(BF16)
    )


def match_kernel(
    anchors_ref, recv_ref, images_ref, above_ref, below_ref,
    columns_ref, rows_ref, left_ref, right_ref, out_ref,
    framed_ref, facts_ref, whole_ref, scalar_ref, list_ref, data_ref, section_ref,
    energy_ref, tall_ref, wide_ref, copy_sem,
):
    blocks = recv_ref.shape[0]
    dates = images_ref.shape[0]
    facts_ref[...] = recv_ref[:, 2 * CHIP : 2 * CHIP + 8, :].astype(F32).reshape(blocks * 8, LANES)
    whole_ref[...] = jnp.zeros(whole_ref.shape, jnp.int32)
    for rank in range(2):
        whole_ref[rank * blocks : (rank + 1) * blocks, :] = facts_ref[
            pl.ds(rank, blocks, stride=8), :
        ].astype(jnp.int32)
    copy = pltpu.make_async_copy(whole_ref, scalar_ref, copy_sem)
    copy.start()
    framed_ref[:, :SMAX, :] = above_ref[...].astype(F32)
    framed_ref[:, SMAX : SMAX + CHIP, :] = images_ref[...].astype(F32)
    framed_ref[:, SMAX + CHIP :, :] = below_ref[...].astype(F32)
    for ref in (energy_ref, tall_ref, wide_ref):
        ref[...] = jnp.zeros(ref.shape, F32)
    copy.wait()

    def note(slot, count):
        list_ref[count] = slot
        return count + scalar_ref[slot, 0]

    count = lax.fori_loop(0, 2 * blocks, note, 0)
    spare = 2 * CHIP // 2
    for extra in range(BATCH):
        list_ref[count + extra] = spare
    lane = lax.broadcasted_iota(jnp.int32, (1, LANES), 1)
    low = lane < CHIP
    ones = same_chip()

    def one_batch(turn, carry):
        rows_of = []
        windows = []
        for s in range(BATCH):
            slot = list_ref[turn * BATCH + s]
            rows_of.append(slot)
            source = jnp.where(slot == spare, 0, slot)
            rank = jnp.where(source >= blocks, 1, 0)
            second = scalar_ref[slot, 1]
            pieces = []
            starts = []
            for chip in range(2):
                down = scalar_ref[slot, 3 + 2 * chip] + SMAX
                start = scalar_ref[slot, 4 + 2 * chip] + anchors_ref[chip] - chip * CHIP
                piece = framed_ref[second, pl.ds(down, CHIP), :]
                pieces.append(pltpu.roll(piece, lax.rem(LANES - start, LANES), 1))
                starts.append(start)
            column = lane + jnp.where(low, starts[0], starts[1])
            inside = (column >= 0) & (column < LANES)
            window = jnp.where(low, pieces[0], pieces[1])
            windows.append(jnp.where(inside, window, 0.0))
            data_ref[s * 2 * CHIP : s * 2 * CHIP + CHIP, :] = recv_ref[
                source - rank * blocks, pl.ds(pl.multiple_of(rank * CHIP, CHIP), CHIP), :
            ]
        sums = [jnp.sum(w, axis=0, keepdims=True) for w in windows]
        sums += [jnp.zeros((1, LANES), F32)] * (8 - BATCH)
        means = dot(jnp.concatenate(sums, axis=0), ones, HIGH) * (1.0 / (CHIP * CHIP))
        for s in range(BATCH):
            data_ref[s * 2 * CHIP + CHIP : (s + 1) * 2 * CHIP, :] = (
                windows[s] - means[s : s + 1]
            ).astype(BF16)
        section_ref[...] = dot(data_ref[...], columns_ref[...]).astype(BF16)
        for s in range(BATCH):
            near = section_ref[s * 2 * CHIP : s * 2 * CHIP + CHIP, :]
            far = section_ref[s * 2 * CHIP + CHIP : (s + 1) * 2 * CHIP, :]
            real = jnp.concatenate([near[:, :LANES], far[:, :LANES]], axis=1)
            imag = jnp.concatenate([near[:, LANES:], far[:, LANES:]], axis=1)
            spectrum = dot(rows_ref[...], jnp.concatenate([real, imag], axis=0))
            near_re, far_re = spectrum[:CHIP, :LANES], spectrum[:CHIP, LANES:]
            near_im, far_im = spectrum[CHIP:, :LANES], spectrum[CHIP:, LANES:]
            cross_re = near_re * far_re + near_im * far_im
            cross_im = near_im * far_re - near_re * far_im
            short_re, short_im = cross_re.astype(BF16), cross_im.astype(BF16)
            tall = dot(left_ref[...], jnp.concatenate([short_re, short_im], axis=0))
            wide = dot(jnp.concatenate([short_re, short_im], axis=1), right_ref[...])
            power = cross_re * cross_re + cross_im * cross_im
            tall = cross_re * tall[:CHIP] + cross_im * tall[CHIP:]
            wide = cross_re * wide[:, :LANES] + cross_im * wide[:, LANES:]
            half = CHIP // 2
            middle = jnp.where(lane % CHIP == half, 0.0, 0.5 * power[half : half + 1])
            at = pl.ds(rows_of[s], 1)
            energy_ref[at, :] = jnp.sum(power, axis=0, keepdims=True) - middle
            tall_ref[at, :] = jnp.sum(tall, axis=0, keepdims=True)
            wide_ref[at, :] = jnp.sum(wide, axis=0, keepdims=True) - 0.5 * wide[half : half + 1]
        return carry

    lax.fori_loop(0, (count + BATCH - 1) // BATCH, one_batch, 0)

    lane8 = lax.broadcasted_iota(jnp.int32, (8, LANES), 1)
    row8 = lax.broadcasted_iota(jnp.int32, (8, LANES), 0)
    weights = jnp.where((row8 == 0) & (lane8 % CHIP == CHIP // 2), 0.5, 1.0)
    stack = []
    for ref in (energy_ref, tall_ref, wide_ref):
        value = ref[:CHIP, :]
        stack += [jnp.where(low, value, 0.0), jnp.where(low, 0.0, value)]
    found = dot_nt(weights, jnp.concatenate(stack, axis=0), HIGH)
    norm = found[0:1, :LANES] + 1e-6
    tall = found[0:1, LANES : 2 * LANES] / norm
    wide = found[1:2, 2 * LANES :] / norm
    whole = whole_ref[:CHIP, :].astype(F32).astype(BF16)
    choose = (lane8 == row8).astype(F32).astype(BF16)
    fact = dot_nt(choose, jnp.concatenate([whole, whole], axis=0))
    live = fact[0:1] > 0.5
    down = jnp.where(live, jnp.where(low, fact[3:4], fact[5:6]) + tall, 0.0)
    across = jnp.where(live, jnp.where(low, fact[4:5], fact[6:7]) + wide, 0.0)
    row = lax.broadcasted_iota(jnp.int32, (LANES, LANES), 0).astype(F32)
    base = (lax.rem(lax.axis_index("date"), LANES // dates) * dates).astype(F32)
    chosen = (row == fact[1:2] + base).astype(F32)
    value = jnp.where(row8 < 6, down, across)
    value = jnp.where((row8 >= 4) & ((row8 % 2 == 0) == (lane8 < CHIP)), value, 0.0)
    result = dot_nt(value, chosen, HIGH)
    result = jnp.where(row8 == 0, down, result)
    result = jnp.where(row8 == 1, across, result)
    result = jnp.where(row8 == 2, fact[2:3], result)
    for block in range(blocks):
        out_ref[block] = result


def series_kernel(
    block_ref, count_ref, result_ref, inverse_ref, turned_ref, offsets_ref, series_ref, tally_ref
):
    blocks = result_ref.shape[0]
    slots = block_ref.shape[0]
    dates = inverse_ref.shape[2]
    me = lax.axis_index("date")
    lane8 = lax.broadcasted_iota(jnp.int32, (8, LANES), 1)
    for block in range(blocks):
        tally_ref[block] = 0
    for slot in range(slots):
        block = block_ref[slot, 0]
        rank = tally_ref[block]
        tally_ref[block] = rank + 1
        turn = rank * blocks + me
        value = pltpu.roll(result_ref[block], lax.rem(2 * LANES - turn, LANES), 1)
        other = pltpu.roll(value, LANES - CHIP + 1, 1)
        value = jnp.where(lane8 == 0, value, other)
        value = jnp.where(slot < count_ref[0], value, 0.0)
        offsets_ref[slot] = value[:2, :2]
    sums = [jnp.zeros((8, LANES), F32) for _ in range(dates)]
    per = LANES // dates
    groups = [jnp.zeros((8, LANES), F32) for _ in range(blocks // per)]
    for block in range(blocks):
        value = result_ref[block]
        first = jnp.broadcast_to(value[2:3], (8, LANES))
        for date in range(dates):
            sums[date] = sums[date] + jnp.where(first == date, value, 0.0)
        groups[block // per] = groups[block // per] + value
    low = lax.broadcasted_iota(jnp.int32, (dates, LANES), 1) < CHIP
    ones = jnp.ones((8, LANES), F32)
    for axis in range(2):
        own = jnp.zeros((dates, LANES), F32)
        for date in range(dates):
            own = own + turned_ref[axis, date] * sums[date][axis : axis + 1]
        for chip in range(2):
            total = jnp.where(low if chip == 0 else ~low, -own, 0.0)
            at = 4 + 2 * axis + chip
            for g, group in enumerate(groups):
                total = total + inverse_ref[axis, chip, :, g * LANES : (g + 1) * LANES] * group[at : at + 1]
            series_ref[axis, chip : chip + 1, :] = dot_nt(ones, total, HIGH)[0:1, :]


def body(images, inverse_blocks, pair_first, pair_block, pair_second, pair_count, shifts, anchors):
    blocks = lax.axis_size("date")
    strips = lax.axis_size("strip")
    dates, length, columns = images.shape
    slots = pair_first.shape[0]
    smem = pl.BlockSpec(memory_space=pltpu.SMEM)
    vmem = pl.BlockSpec(memory_space=pltpu.VMEM)
    params = pltpu.CompilerParams(vmem_limit_bytes=48 * 2**20)
    ends = strips - 1
    above = lax.ppermute(
        images[:, length - SMAX :, :], "strip", [(i, i + 1) for i in range(ends)]
    )
    below = lax.ppermute(images[:, :SMAX, :], "strip", [(i + 1, i) for i in range(ends)])
    send = pl.pallas_call(
        pack_kernel,
        out_shape=jax.ShapeDtypeStruct((blocks, 2 * length + 8, columns), BF16),
        in_specs=[smem] * 6 + [vmem],
        out_specs=vmem,
        scratch_shapes=[
            pltpu.VMEM((dates, length, columns), F32),
            pltpu.VMEM((dates, length, columns), BF16),
            pltpu.VMEM((blocks * 8, columns), F32),
            pltpu.SMEM((blocks,), jnp.int32),
        ],
        compiler_params=params,
    )(pair_first, pair_block, pair_second, pair_count, shifts, anchors, images)
    recv = lax.all_to_all(send, "date", split_axis=0, concat_axis=0, tiled=True)
    tables = make_tables()
    result = pl.pallas_call(
        match_kernel,
        out_shape=jax.ShapeDtypeStruct((blocks, 8, columns), F32),
        in_specs=[smem] + [vmem] * 8,
        out_specs=vmem,
        scratch_shapes=[
            pltpu.VMEM((dates, length + 2 * SMAX, columns), F32),
            pltpu.VMEM((blocks * 8, columns), F32),
            pltpu.VMEM((CHIP + 8, columns), jnp.int32),
            pltpu.SMEM((CHIP + 8, columns), jnp.int32),
            pltpu.SMEM((CHIP + 8,), jnp.int32),
            pltpu.VMEM((BATCH * 2 * length, columns), BF16),
            pltpu.VMEM((BATCH * 2 * length, 2 * columns), BF16),
            pltpu.VMEM((CHIP + 8, columns), F32),
            pltpu.VMEM((CHIP + 8, columns), F32),
            pltpu.VMEM((CHIP + 8, columns), F32),
            pltpu.SemaphoreType.DMA,
        ],
        compiler_params=params,
    )(anchors, recv, images, above, below, *[jnp.asarray(t) for t in tables])
    result = lax.all_to_all(result, "date", split_axis=0, concat_axis=0, tiled=True)
    turned = inverse_blocks.reshape(2, 2, dates, blocks, dates).transpose(0, 4, 2, 1, 3)
    turned = jnp.concatenate([turned, turned], axis=4)
    turned = jnp.pad(turned, ((0, 0),) * 4 + ((0, CHIP - 2 * blocks),))
    turned = turned.reshape(2, dates, dates, LANES)
    return pl.pallas_call(
        series_kernel,
        out_shape=(
            jax.ShapeDtypeStruct((slots, 2, 2), F32),
            jax.ShapeDtypeStruct((2, 2, dates), F32),
        ),
        in_specs=[smem] * 2 + [vmem] * 3,
        out_specs=(vmem, vmem),
        scratch_shapes=[pltpu.SMEM((blocks,), jnp.int32)],
        compiler_params=params,
    )(pair_block, pair_count, result, inverse_blocks, turned)


def solution(mesh):
    return jax.shard_map(
        body,
        mesh=mesh,
        in_specs=(
            P("date", "strip", None),
            P(None, "strip", "date", None),
            P("date"),
            P("date", None),
            P("date"),
            P("date"),
            P("date", None, "strip"),
            P("strip"),
        ),
        out_specs=(P("date", None, "strip"), P(None, "strip", "date")),
        check_vma=False,
    )
```

```python
import math

import jax
import jax.numpy as jnp
import ml_dtypes
import numpy as np
from jax import lax
from jax.experimental import pallas as pl
from jax.experimental.pallas import tpu as pltpu
from jax.sharding import PartitionSpec as P

SMAX = 8
CHIP = 64
LANES = 128
BATCH = 8
HIGH = lax.Precision.HIGHEST
F32 = jnp.float32
BF16 = jnp.bfloat16


def make_tables():
    half = CHIP // 2
    counter = np.arange(CHIP)
    freq = counter % half
    def basis(places, length):
        turn = 2.0 * math.pi * freq[:, None] * places[None, :] / length
        value = np.where(counter[:, None] < half, np.cos(turn), np.sin(turn))
        value[half] = np.cos(2.0 * math.pi * half * places / length)
        return value
    scale = np.where(freq == 0, 1.0, math.sqrt(2.0))[:, None]
    forward = basis(counter, CHIP) * scale
    cosine, sine = forward[:half].T, forward[half:].T
    zero = np.zeros((CHIP, half))
    def spread(block):
        return np.concatenate([np.concatenate([block, zero], 1), np.concatenate([zero, block], 1)], 0)
    nyquist = cosine.copy(); nyquist[:, 0] = sine[:, 0]
    plain = sine.copy(); plain[:, 0] = 0.0
    near = np.concatenate([spread(cosine), spread(sine)], 1)
    far = np.concatenate([spread(cosine), spread(nyquist), spread(plain), spread(plain)], 1)
    places = np.arange(2 * CHIP)
    displace = ((places + CHIP) % (2 * CHIP) - CHIP) * 0.5
    wave = basis(places, 2 * CHIP)
    form = (wave * displace) @ wave.T / (2 * CHIP)
    cc, cs, sc, ss = form[:half, :half], form[:half, half:], form[half:, :half], form[half:, half:]
    two = np.eye(2)
    across = np.block([[np.kron(two, cc), np.kron(two, cs)], [np.kron(two, sc), np.kron(two, ss)]])
    tables = (near, far, forward, form, across)
    return tuple(a.astype(ml_dtypes.bfloat16) for a in tables)


def dot(a, b, precision=None):
    return lax.dot_general(
        a, b, (((1,), (0,)), ((), ())), precision=precision, preferred_element_type=F32
    )


def dot_nt(a, b, precision=None):
    return lax.dot_general(
        a, b, (((1,), (1,)), ((), ())), precision=precision, preferred_element_type=F32
    )


def level_lanes():
    lane = lax.broadcasted_iota(jnp.int32, (1, LANES), 1)
    return jnp.where((lane < CHIP) & (lane % (CHIP // 2) == 0), 1.0 / CHIP, 0.0)


def pack_kernel(
    first_hbm, block_hbm, second_hbm, count_hbm, shifts_hbm, anchors_hbm, images_hbm,
    table_ref, forward_ref,
    send_ref, own_ref, images_ref,
    first_ref, block_ref, second_ref, count_ref, shifts_ref, anchors_ref,
    near_ref, facts_ref, tally_ref, sems,
):
    dates = images_ref.shape[0]
    blocks = send_ref.shape[0]
    slots = first_ref.shape[0]
    copies = [
        pltpu.make_async_copy(source, target, sems.at[index])
        for index, (source, target) in enumerate(
            (
                (anchors_hbm, anchors_ref), (first_hbm, first_ref), (block_hbm, block_ref),
                (second_hbm, second_ref), (count_hbm, count_ref), (shifts_hbm, shifts_ref),
                (images_hbm, images_ref),
            )
        )
    ]
    for copy in copies:
        copy.start()
    facts_ref[...] = jnp.zeros(facts_ref.shape, F32)
    for block in range(blocks):
        tally_ref[block] = 0
    row = lax.broadcasted_iota(jnp.int32, (LANES, LANES), 0)
    lane = lax.broadcasted_iota(jnp.int32, (LANES, LANES), 1)
    for copy in copies:
        copy.wait()
    column = lane + jnp.where(lane < CHIP, anchors_ref[0], anchors_ref[1] - CHIP)
    pick = (row == column).astype(F32).astype(BF16)
    table = dot(pick, table_ref[...]).astype(BF16)
    section = dot(images_ref[...].reshape(dates * CHIP, LANES), table)
    level = level_lanes()
    parts = []
    for date in range(dates):
        part = section[date * CHIP : (date + 1) * CHIP]
        parts.append((part - level * jnp.sum(part, axis=0, keepdims=True)).astype(BF16))
    for date in range(0, dates, 2):
        pair = dot(forward_ref[...], jnp.concatenate(parts[date : date + 2], axis=1)).astype(BF16)
        near_ref[date] = pair[:, :LANES]
        near_ref[date + 1] = pair[:, LANES:]
    place = lax.broadcasted_iota(jnp.int32, (1, LANES), 1)
    for slot in range(slots):
        block = block_ref[slot]
        rank = tally_ref[block]
        tally_ref[block] = rank + 1
        live = jnp.where(slot < count_ref[0], 1, 0)
        first = first_ref[slot]
        at = pl.multiple_of(rank * CHIP, CHIP)
        send_ref[block, pl.ds(at, CHIP), :] = near_ref[first]
        fact = jnp.where(place == 0, live, 0)
        values = [second_ref[slot], first]
        for chip in range(2):
            values += [shifts_ref[0, chip, slot], shifts_ref[1, chip, slot]]
        for chip in range(2):
            values += [shifts_ref[1, chip, slot] + anchors_ref[chip] - chip * CHIP]
        for index, value in enumerate(values):
            fact = jnp.where(place == index + 1, value, fact)
        facts_ref[pl.ds(block * 8 + rank, 1), :] = fact.astype(F32)
        own = jnp.where(place == 0, block, jnp.where(live > 0, rank * blocks, -1))
        own_ref[slot : slot + 1, :] = own.astype(F32)
    send_ref[:, 2 * CHIP : 2 * CHIP + 8, :] = (
        facts_ref[...].reshape(blocks, 8, LANES).astype(BF16)
    )


def match_kernel(
    recv_ref, images_ref, above_ref, below_ref,
    table_ref, forward_ref, form_ref, across_ref, out_ref,
    framed_ref, facts_ref, whole_ref, scalar_ref, list_ref, data_ref, cross_ref,
    energy_ref, tall_ref, wide_ref, copy_sem,
):
    blocks = recv_ref.shape[0]
    dates = images_ref.shape[0]
    half = CHIP // 2
    facts_ref[...] = recv_ref[:, 2 * CHIP : 2 * CHIP + 8, :].astype(F32).reshape(blocks * 8, LANES)
    whole_ref[...] = jnp.zeros(whole_ref.shape, jnp.int32)
    for rank in range(2):
        whole_ref[rank * blocks : (rank + 1) * blocks, :] = facts_ref[
            pl.ds(rank, blocks, stride=8), :
        ].astype(jnp.int32)
    copy = pltpu.make_async_copy(whole_ref, scalar_ref, copy_sem)
    copy.start()
    framed_ref[:, :SMAX, :] = above_ref[...].astype(F32)
    framed_ref[:, SMAX : SMAX + CHIP, :] = images_ref[...].astype(F32)
    framed_ref[:, SMAX + CHIP :, :] = below_ref[...].astype(F32)
    for ref in (energy_ref, tall_ref, wide_ref):
        ref[...] = jnp.zeros(ref.shape, F32)
    copy.wait()

    def note(slot, count):
        list_ref[count] = slot
        return count + scalar_ref[slot, 0]

    count = lax.fori_loop(0, 2 * blocks, note, 0)
    spare = 2 * CHIP // 2
    for extra in range(BATCH):
        list_ref[count + extra] = spare
    lane = lax.broadcasted_iota(jnp.int32, (1, LANES), 1)
    low = lane < CHIP
    level = level_lanes()
    turn_sign = jnp.where(lane % half == 0, 0.0, jnp.where(low, 1.0, -1.0))
    corner = jnp.where((lane % half == 0) & (lane >= CHIP), 1.0, 0.0)
    top_row = lax.broadcasted_iota(jnp.int32, (8, LANES), 0) == 0

    def one_batch(turn, carry):
        rows_of = []
        near_of = []
        for s in range(BATCH):
            slot = list_ref[turn * BATCH + s]
            rows_of.append(slot)
            source = jnp.where(slot == spare, 0, slot)
            rank = jnp.where(source >= blocks, 1, 0)
            near_of.append((source - rank * blocks, pl.multiple_of(rank * CHIP, CHIP)))
            second = scalar_ref[slot, 1]
            pieces = []
            starts = []
            for chip in range(2):
                down = scalar_ref[slot, 3 + 2 * chip] + SMAX
                start = scalar_ref[slot, 7 + chip]
                piece = framed_ref[second, pl.ds(down, CHIP), :]
                pieces.append(pltpu.roll(piece, lax.rem(LANES - start, LANES), 1))
                starts.append(start)
            column = lane + jnp.where(low, starts[0], starts[1])
            inside = (column >= 0) & (column < LANES)
            window = jnp.where(low, pieces[0], pieces[1])
            data_ref[s * CHIP : (s + 1) * CHIP, :] = jnp.where(inside, window, 0.0).astype(BF16)
        section = dot(data_ref[...], table_ref[...])
        crosses = []
        for s in range(BATCH):
            part = section[s * CHIP : (s + 1) * CHIP, :LANES]
            part = part - level * jnp.sum(part, axis=0, keepdims=True)
            other = section[s * CHIP : (s + 1) * CHIP, LANES:]
            far = dot(forward_ref[...], jnp.concatenate([part, other], axis=1).astype(BF16))
            block, at = near_of[s]
            near = recv_ref[block, pl.ds(at, CHIP), :].astype(F32)
            turned = pltpu.roll(near, CHIP, 1) * turn_sign
            top, low_rows = near[:half], near[half:]
            top_turned, low_turned = turned[:half], turned[half:]
            p, q = far[:half, :LANES], far[:half, LANES:]
            p_low, q_low = far[half:, :LANES], far[half:, LANES:]
            first = top * p + top_turned * q
            second = low_rows * p_low + low_turned * q_low
            upper = first + second
            lower = (low_rows * p + low_turned * q) - (top * p_low + top_turned * q_low)
            upper = jnp.concatenate([jnp.where(top_row, first[:8], upper[:8]), upper[8:]], axis=0)
            lower = jnp.concatenate([jnp.where(top_row, second[:8], lower[:8]), lower[8:]], axis=0)
            cross = jnp.concatenate([upper, lower], axis=0)
            crosses.append(cross)
            cross_ref[s * CHIP : (s + 1) * CHIP, :] = cross.astype(BF16)
        wide = dot(cross_ref[...], across_ref[...])
        for s in range(0, BATCH, 2):
            pair = [cross_ref[r * CHIP : (r + 1) * CHIP, :] for r in (s, s + 1)]
            tall = dot(form_ref[...], jnp.concatenate(pair, axis=1))
            for r in range(2):
                cross = crosses[s + r]
                power = cross * cross
                tall_r = cross * tall[:, r * LANES : (r + 1) * LANES]
                wide_r = cross * wide[(s + r) * CHIP : (s + r + 1) * CHIP]
                at = pl.ds(rows_of[s + r], 1)
                energy_ref[at, :] = 0.5 * (
                    jnp.sum(power, axis=0, keepdims=True)
                    + power[:1] + corner * power[half : half + 1]
                )
                tall_ref[at, :] = jnp.sum(tall_r, axis=0, keepdims=True)
                wide_ref[at, :] = 0.5 * (jnp.sum(wide_r, axis=0, keepdims=True) + wide_r[:1])
        return carry

    lax.fori_loop(0, (count + BATCH - 1) // BATCH, one_batch, 0)

    lane8 = lax.broadcasted_iota(jnp.int32, (8, LANES), 1)
    row8 = lax.broadcasted_iota(jnp.int32, (8, LANES), 0)
    weights = jnp.where((row8 == 1) | ((lane8 % half == 0) & (lane8 < CHIP)), 1.0, 0.5)
    even = lane // half % 2 == 0
    stack = []
    for ref in (energy_ref, tall_ref, wide_ref):
        value = ref[:CHIP, :]
        stack += [jnp.where(even, value, 0.0), jnp.where(even, 0.0, value)]
    found = dot_nt(weights, jnp.concatenate(stack, axis=0), HIGH)
    norm = found[0:1, :LANES] + 1e-6
    tall = found[0:1, LANES : 2 * LANES] / norm
    wide = found[1:2, 2 * LANES :] / norm
    whole = whole_ref[:CHIP, :].astype(F32).astype(BF16)
    choose = (lane8 == row8).astype(F32).astype(BF16)
    fact = dot_nt(choose, jnp.concatenate([whole, whole], axis=0))
    live = fact[0:1] > 0.5
    down = jnp.where(live, jnp.where(low, fact[3:4], fact[5:6]) + tall, 0.0)
    across = jnp.where(live, jnp.where(low, fact[4:5], fact[6:7]) + wide, 0.0)
    row = lax.broadcasted_iota(jnp.int32, (LANES, LANES), 0).astype(F32)
    base = (lax.rem(lax.axis_index("date"), LANES // dates) * dates).astype(F32)
    chosen = (row == fact[1:2] + base).astype(F32)
    value = jnp.where(row8 < 6, down, across)
    value = jnp.where((row8 >= 4) & ((row8 % 2 == 0) == (lane8 < CHIP)), value, 0.0)
    result = dot_nt(value, chosen, HIGH)
    result = jnp.where(row8 == 0, down, result)
    result = jnp.where(row8 == 1, across, result)
    result = jnp.where(row8 == 2, fact[2:3], result)
    for block in range(blocks):
        out_ref[block] = result


def series_kernel(
    own_ref, result_ref, inverse_ref, turned_ref, offsets_ref, series_ref
):
    blocks = result_ref.shape[0] // 8
    slots = own_ref.shape[0]
    dates = inverse_ref.shape[2]
    ones = jnp.ones((8, LANES), F32)
    me = lax.axis_index("date").astype(F32)
    own = own_ref[...]
    partner = lax.broadcasted_iota(jnp.int32, (slots, blocks), 1).astype(F32)
    partner = (own[:, 0:1] == partner).astype(F32)
    lane = lax.broadcasted_iota(jnp.int32, (slots, LANES), 1)
    mine = lane.astype(F32) - me == own[:, 1:2] + jnp.where(lane < CHIP, 0.0, float(CHIP))
    mine = mine & (own[:, 1:2] >= 0.0)
    for axis in range(2):
        rows = result_ref[pl.ds(axis, blocks, stride=8), :]
        value = jnp.where(mine, dot(partner, rows, HIGH), 0.0)
        for chip in range(2):
            half = jnp.where(lane < CHIP if chip == 0 else lane >= CHIP, value, 0.0)
            offsets_ref[axis, chip : chip + 1, :] = dot_nt(ones, half, HIGH)[0:1, :]
    sums = [jnp.zeros((8, LANES), F32) for _ in range(dates)]
    per = LANES // dates
    groups = [jnp.zeros((8, LANES), F32) for _ in range(blocks // per)]
    for block in range(blocks):
        value = result_ref[block * 8 : block * 8 + 8, :]
        first = jnp.broadcast_to(value[2:3], (8, LANES))
        for date in range(dates):
            sums[date] = sums[date] + jnp.where(first == date, value, 0.0)
        groups[block // per] = groups[block // per] + value
    low = lax.broadcasted_iota(jnp.int32, (dates, LANES), 1) < CHIP
    for axis in range(2):
        own = jnp.zeros((dates, LANES), F32)
        for date in range(dates):
            own = own + turned_ref[axis, date] * sums[date][axis : axis + 1]
        for chip in range(2):
            total = jnp.where(low if chip == 0 else ~low, -own, 0.0)
            at = 4 + 2 * axis + chip
            for g, group in enumerate(groups):
                total = total + inverse_ref[axis, chip, :, g * LANES : (g + 1) * LANES] * group[at : at + 1]
            series_ref[axis, chip : chip + 1, :] = dot_nt(ones, total, HIGH)[0:1, :]


def body(images, inverse_blocks, pair_first, pair_block, pair_second, pair_count, shifts, anchors):
    blocks = lax.axis_size("date")
    strips = lax.axis_size("strip")
    dates, length, columns = images.shape
    slots = pair_first.shape[0]
    hbm = pl.BlockSpec(memory_space=pltpu.HBM)
    vmem = pl.BlockSpec(memory_space=pltpu.VMEM)
    params = pltpu.CompilerParams(vmem_limit_bytes=48 * 2**20)
    ends = strips - 1
    above = lax.ppermute(
        images[:, length - SMAX :, :], "strip", [(i, i + 1) for i in range(ends)]
    )
    below = lax.ppermute(images[:, :SMAX, :], "strip", [(i + 1, i) for i in range(ends)])
    turned = inverse_blocks.reshape(2, 2, dates, blocks, dates).transpose(0, 4, 2, 1, 3)
    turned = jnp.concatenate([turned, turned], axis=4)
    turned = jnp.pad(turned, ((0, 0),) * 4 + ((0, CHIP - 2 * blocks),))
    turned = turned.reshape(2, dates, dates, LANES)
    near_table, far_table, forward, form, across = [jnp.asarray(t) for t in make_tables()]
    send, own = pl.pallas_call(
        pack_kernel,
        out_shape=(
            jax.ShapeDtypeStruct((blocks, 2 * length + 8, columns), BF16),
            jax.ShapeDtypeStruct((slots, columns), F32),
        ),
        in_specs=[hbm] * 7 + [vmem] * 2,
        out_specs=(vmem, vmem),
        scratch_shapes=[
            pltpu.VMEM(images.shape, BF16),
            pltpu.SMEM((slots,), jnp.int32),
            pltpu.SMEM((slots,), jnp.int32),
            pltpu.SMEM((slots,), jnp.int32),
            pltpu.SMEM((1,), jnp.int32),
            pltpu.SMEM((2, 2, slots), jnp.int32),
            pltpu.SMEM((2,), jnp.int32),
            pltpu.VMEM((dates, length, columns), BF16),
            pltpu.VMEM((blocks * 8, columns), F32),
            pltpu.SMEM((blocks,), jnp.int32),
            pltpu.SemaphoreType.DMA((7,)),
        ],
        compiler_params=pltpu.CompilerParams(vmem_limit_bytes=60 * 2**20),
    )(
        pair_first, pair_block[:, 0], pair_second, pair_count,
        jnp.transpose(shifts, (1, 2, 0)), anchors, images, near_table, forward,
    )
    recv = lax.all_to_all(send, "date", split_axis=0, concat_axis=0, tiled=True)
    recv, turned = lax.optimization_barrier((recv, turned))
    result = pl.pallas_call(
        match_kernel,
        out_shape=jax.ShapeDtypeStruct((blocks, 8, columns), F32),
        in_specs=[vmem] * 8,
        out_specs=vmem,
        scratch_shapes=[
            pltpu.VMEM((dates, length + 2 * SMAX, columns), F32),
            pltpu.VMEM((blocks * 8, columns), F32),
            pltpu.VMEM((CHIP + 8, columns), jnp.int32),
            pltpu.SMEM((CHIP + 8, columns), jnp.int32),
            pltpu.SMEM((CHIP + BATCH,), jnp.int32),
            pltpu.VMEM((BATCH * length, columns), BF16),
            pltpu.VMEM((BATCH * length, columns), BF16),
            pltpu.VMEM((CHIP + 8, columns), F32),
            pltpu.VMEM((CHIP + 8, columns), F32),
            pltpu.VMEM((CHIP + 8, columns), F32),
            pltpu.SemaphoreType.DMA,
        ],
        compiler_params=params,
    )(recv, images, above, below, far_table, forward, form, across)
    result = lax.all_to_all(result, "date", split_axis=0, concat_axis=0, tiled=True)
    offsets, series = pl.pallas_call(
        series_kernel,
        out_shape=(
            jax.ShapeDtypeStruct((2, 2, slots), F32),
            jax.ShapeDtypeStruct((2, 2, dates), F32),
        ),
        in_specs=[vmem] * 4,
        out_specs=(vmem, vmem),
        compiler_params=params,
    )(own, result.reshape(blocks * 8, columns), inverse_blocks, turned)
    return jnp.transpose(offsets, (2, 0, 1)), series


def solution(mesh):
    return jax.shard_map(
        body,
        mesh=mesh,
        in_specs=(
            P("date", "strip", None),
            P(None, "strip", "date", None),
            P("date"),
            P("date", None),
            P("date"),
            P("date"),
            P("date", None, "strip"),
            P("strip"),
        ),
        out_specs=(P("date", None, "strip"), P(None, "strip", "date")),
        check_vma=False,
    )
```

```python
import math

import jax
import jax.numpy as jnp
import ml_dtypes
import numpy as np
from jax import lax
from jax.experimental import pallas as pl
from jax.experimental.pallas import tpu as pltpu
from jax.sharding import PartitionSpec as P

SMAX = 8
CHIP = 64
LANES = 128
BATCH = 16
F32 = jnp.float32
BF16 = jnp.bfloat16


def make_tables():
    half = CHIP // 2
    counter = np.arange(CHIP)
    freq = counter % half
    def basis(places, length):
        turn = 2.0 * math.pi * freq[:, None] * places[None, :] / length
        value = np.where(counter[:, None] < half, np.cos(turn), np.sin(turn))
        value[half] = np.cos(2.0 * math.pi * half * places / length)
        return value
    scale = np.where(freq == 0, 1.0, math.sqrt(2.0))[:, None]
    forward = basis(counter, CHIP) * scale
    cosine, sine = forward[:half].T, forward[half:].T
    zero = np.zeros((CHIP, half))
    def spread(block):
        return np.concatenate([np.concatenate([block, zero], 1), np.concatenate([zero, block], 1)], 0)
    nyquist = cosine.copy(); nyquist[:, 0] = sine[:, 0]
    plain = sine.copy(); plain[:, 0] = 0.0
    near = np.concatenate([spread(cosine), spread(sine)], 1)
    far = np.concatenate([spread(cosine), spread(nyquist), spread(plain), spread(plain)], 1)
    places = np.arange(2 * CHIP)
    displace = ((places + CHIP) % (2 * CHIP) - CHIP) * 0.5
    wave = basis(places, 2 * CHIP)
    form = (wave * displace) @ wave.T / (2 * CHIP)
    cc, cs, sc, ss = form[:half, :half], form[:half, half:], form[half:, :half], form[half:, half:]
    two = np.eye(2)
    across = np.block([[np.kron(two, cc), np.kron(two, cs)], [np.kron(two, sc), np.kron(two, ss)]])
    tables = (near, far, forward, form, across)
    return tuple(a.astype(ml_dtypes.bfloat16) for a in tables)


def dot(a, b):
    return lax.dot_general(a, b, (((1,), (0,)), ((), ())), preferred_element_type=F32)


def dot_nt(a, b):
    return lax.dot_general(a, b, (((1,), (1,)), ((), ())), preferred_element_type=F32)


def parts_of(value, count):
    parts = []
    for _ in range(count):
        part = value.astype(BF16)
        parts.append(part)
        value = value - part.astype(F32)
    return parts


def level_lanes():
    lane = lax.broadcasted_iota(jnp.int32, (1, LANES), 1)
    return jnp.where((lane < CHIP) & (lane % (CHIP // 2) == 0), 1.0 / CHIP, 0.0)


def pack_kernel(
    first_hbm, block_hbm, second_hbm, count_hbm, shifts_hbm, anchors_hbm, images_hbm,
    table_ref, forward_ref,
    send_ref, own_ref, images_ref,
    first_ref, block_ref, second_ref, count_ref, shifts_ref, anchors_ref,
    near_ref, facts_ref, tally_ref, where_ref, sems,
):
    dates = images_ref.shape[0]
    blocks = send_ref.shape[0]
    slots = first_ref.shape[0]
    copies = [
        pltpu.make_async_copy(source, target, sems.at[index])
        for index, (source, target) in enumerate(
            (
                (anchors_hbm, anchors_ref), (first_hbm, first_ref), (block_hbm, block_ref),
                (second_hbm, second_ref), (count_hbm, count_ref), (shifts_hbm, shifts_ref),
                (images_hbm, images_ref),
            )
        )
    ]
    for copy in copies:
        copy.start()
    facts_ref[...] = jnp.zeros(facts_ref.shape, F32)
    for block in range(blocks):
        tally_ref[block] = 0
    for copy in copies[:-1]:
        copy.wait()
    place = lax.broadcasted_iota(jnp.int32, (1, LANES), 1)
    for slot in range(slots):
        block = block_ref[slot]
        rank = tally_ref[block]
        tally_ref[block] = rank + 1
        where_ref[slot] = rank
        live = jnp.where(slot < count_ref[0], 1, 0)
        values = [live, second_ref[slot]]
        for chip in range(2):
            start = shifts_ref[1, chip, slot] + anchors_ref[chip] - chip * CHIP
            values += [shifts_ref[0, chip, slot], start]
        values += [first_ref[slot], shifts_ref[1, 0, slot], shifts_ref[1, 1, slot]]
        fact = jnp.zeros((1, LANES), jnp.int32)
        for index, value in enumerate(values):
            fact = jnp.where(place == index, value, fact)
        facts_ref[pl.ds(block * 8 + rank, 1), :] = fact.astype(F32)
        own = jnp.where(place == 0, block, jnp.where(live > 0, rank * blocks, -1))
        own_ref[slot : slot + 1, :] = own.astype(F32)
    row = lax.broadcasted_iota(jnp.int32, (LANES, LANES), 0)
    lane = lax.broadcasted_iota(jnp.int32, (LANES, LANES), 1)
    column = lane + jnp.where(lane < CHIP, anchors_ref[0], anchors_ref[1] - CHIP)
    pick = (row == column).astype(F32).astype(BF16)
    table = dot(pick, table_ref[...]).astype(BF16)
    level = level_lanes()
    copies[-1].wait()
    section = dot(images_ref[...].reshape(dates * CHIP, LANES), table)
    parts = []
    for date in range(dates):
        part = section[date * CHIP : (date + 1) * CHIP]
        parts.append((part - level * jnp.sum(part, axis=0, keepdims=True)).astype(BF16))
    for date in range(0, dates, 2):
        pair = dot(forward_ref[...], jnp.concatenate(parts[date : date + 2], axis=1)).astype(BF16)
        near_ref[date] = pair[:, :LANES]
        near_ref[date + 1] = pair[:, LANES:]
    for slot in range(slots):
        at = pl.multiple_of(where_ref[slot] * CHIP, CHIP)
        send_ref[block_ref[slot], pl.ds(at, CHIP), :] = near_ref[first_ref[slot]]
    send_ref[:, 2 * CHIP : 2 * CHIP + 8, :] = (
        facts_ref[...].reshape(blocks, 8, LANES).astype(BF16)
    )


def match_kernel(
    recv_ref, images_ref, above_ref, below_ref,
    table_ref, forward_ref, form_ref, across_ref, out_ref,
    framed_ref, facts_ref, whole_ref, scalar_ref, list_ref, data_ref, cross_ref,
    energy_ref, tall_ref, wide_ref, copy_sem,
):
    blocks = recv_ref.shape[0]
    dates = images_ref.shape[0]
    half = CHIP // 2
    facts_ref[...] = recv_ref[:, 2 * CHIP : 2 * CHIP + 8, :].astype(F32).reshape(blocks * 8, LANES)
    whole = [facts_ref[pl.ds(rank, blocks, stride=8), :].astype(BF16) for rank in range(2)]
    if blocks < CHIP // 2:
        whole.append(jnp.zeros((CHIP - 2 * blocks, LANES), BF16))
    lane16 = lax.broadcasted_iota(jnp.int32, (16, LANES), 1)
    row16 = lax.broadcasted_iota(jnp.int32, (16, LANES), 0)
    choose = (lane16 == row16).astype(F32).astype(BF16)
    fact = dot_nt(choose, jnp.concatenate(whole + whole, axis=0))
    whole_ref[...] = fact[:8].astype(jnp.int32)
    copy = pltpu.make_async_copy(whole_ref, scalar_ref, copy_sem)
    copy.start()
    framed_ref[:, :SMAX, :] = above_ref[...].astype(F32)
    framed_ref[:, SMAX : SMAX + CHIP, :] = images_ref[...].astype(F32)
    framed_ref[:, SMAX + CHIP :, :] = below_ref[...].astype(F32)
    for ref in (energy_ref, tall_ref, wide_ref):
        ref[...] = jnp.zeros(ref.shape, F32)
    copy.wait()

    count = 0
    for slot in range(2 * blocks):
        list_ref[count] = slot
        count = count + scalar_ref[0, slot]
    spare = CHIP
    for extra in range(BATCH):
        list_ref[count + extra] = spare
    lane = lax.broadcasted_iota(jnp.int32, (1, LANES), 1)
    low = lane < CHIP
    level = level_lanes()
    turn_sign = jnp.where(lane % half == 0, 0.0, jnp.where(low, 1.0, -1.0))
    corner = jnp.where((lane % half == 0) & (lane >= CHIP), 1.0, 0.0)
    top_row = lax.broadcasted_iota(jnp.int32, (8, LANES), 0) == 0

    def one_batch(turn, carry):
        rows_of = []
        near_of = []
        for s in range(BATCH):
            slot = list_ref[turn * BATCH + s]
            rows_of.append(slot)
            source = jnp.where(slot == spare, 0, slot)
            rank = jnp.where(source >= blocks, 1, 0)
            near_of.append((source - rank * blocks, pl.multiple_of(rank * CHIP, CHIP)))
            second = scalar_ref[1, source]
            pieces = []
            starts = []
            for chip in range(2):
                down = scalar_ref[2 + 2 * chip, source] + SMAX
                start = scalar_ref[3 + 2 * chip, source]
                piece = framed_ref[second, pl.ds(down, CHIP), :]
                pieces.append(pltpu.roll(piece, lax.rem(LANES - start, LANES), 1))
                starts.append(start)
            column = lane + jnp.where(low, starts[0], starts[1])
            inside = (column >= 0) & (column < LANES)
            window = jnp.where(low, pieces[0], pieces[1])
            data_ref[s * CHIP : (s + 1) * CHIP, :] = jnp.where(inside, window, 0.0).astype(BF16)
        section = dot(data_ref[...], table_ref[...])
        crosses = []
        for s in range(BATCH):
            part = section[s * CHIP : (s + 1) * CHIP, :LANES]
            part = part - level * jnp.sum(part, axis=0, keepdims=True)
            other = section[s * CHIP : (s + 1) * CHIP, LANES:]
            far = dot(forward_ref[...], jnp.concatenate([part, other], axis=1).astype(BF16))
            block, at = near_of[s]
            near = recv_ref[block, pl.ds(at, CHIP), :].astype(F32)
            turned = pltpu.roll(near, CHIP, 1) * turn_sign
            top, low_rows = near[:half], near[half:]
            top_turned, low_turned = turned[:half], turned[half:]
            p, q = far[:half, :LANES], far[:half, LANES:]
            p_low, q_low = far[half:, :LANES], far[half:, LANES:]
            first = top * p + top_turned * q
            second = low_rows * p_low + low_turned * q_low
            upper = first + second
            lower = (low_rows * p + low_turned * q) - (top * p_low + top_turned * q_low)
            upper = jnp.concatenate([jnp.where(top_row, first[:8], upper[:8]), upper[8:]], axis=0)
            lower = jnp.concatenate([jnp.where(top_row, second[:8], lower[:8]), lower[8:]], axis=0)
            cross = jnp.concatenate([upper, lower], axis=0)
            crosses.append(cross)
            cross_ref[s * CHIP : (s + 1) * CHIP, :] = cross.astype(BF16)
        wide = dot(cross_ref[...], across_ref[...])
        for s in range(0, BATCH, 2):
            pair = [cross_ref[r * CHIP : (r + 1) * CHIP, :] for r in (s, s + 1)]
            tall = dot(form_ref[...], jnp.concatenate(pair, axis=1))
            for r in range(2):
                cross = crosses[s + r]
                power = cross * cross
                tall_r = cross * tall[:, r * LANES : (r + 1) * LANES]
                wide_r = cross * wide[(s + r) * CHIP : (s + r + 1) * CHIP]
                at = pl.ds(rows_of[s + r], 1)
                energy_ref[at, :] = 0.5 * (
                    jnp.sum(power, axis=0, keepdims=True)
                    + power[:1] + corner * power[half : half + 1]
                )
                tall_ref[at, :] = jnp.sum(tall_r, axis=0, keepdims=True)
                wide_ref[at, :] = 0.5 * (jnp.sum(wide_r, axis=0, keepdims=True) + wide_r[:1])
        return carry

    lax.fori_loop(0, (count + BATCH - 1) // BATCH, one_batch, 0)

    lane8 = lax.broadcasted_iota(jnp.int32, (8, LANES), 1)
    row8 = lax.broadcasted_iota(jnp.int32, (8, LANES), 0)
    weights = jnp.where((row8 == 1) | ((lane8 % half == 0) & (lane8 < CHIP)), 1.0, 0.5)
    even = lane // half % 2 == 0
    stack = []
    for ref in (energy_ref, tall_ref, wide_ref):
        value = ref[:CHIP, :]
        stack += [jnp.where(even, value, 0.0), jnp.where(even, 0.0, value)]
    weights = weights.astype(BF16)
    found = sum(dot_nt(weights, part) for part in parts_of(jnp.concatenate(stack, axis=0), 3))
    norm = found[0:1, :LANES] + 1e-6
    tall = found[0:1, LANES : 2 * LANES] / norm
    wide = found[1:2, 2 * LANES :] / norm
    live = fact[0:1] > 0.5
    down = jnp.where(live, jnp.where(low, fact[2:3], fact[4:5]) + tall, 0.0)
    across = jnp.where(live, jnp.where(low, fact[7:8], fact[8:9]) + wide, 0.0)
    row = lax.broadcasted_iota(jnp.int32, (LANES, LANES), 0).astype(F32)
    base = (lax.rem(lax.axis_index("date"), LANES // dates) * dates).astype(F32)
    chosen = (row == fact[1:2] + base).astype(F32).astype(BF16)
    value = jnp.where(row8 < 6, down, across)
    value = jnp.where((row8 >= 4) & ((row8 % 2 == 0) == (lane8 < CHIP)), value, 0.0)
    result = dot_nt(jnp.concatenate(parts_of(value, 3), axis=0), chosen)
    result = result[:8] + result[8:16] + result[16:24]
    result = jnp.where(row8 == 0, down, result)
    result = jnp.where(row8 == 1, across, result)
    result = jnp.where(row8 == 2, fact[6:7], result)
    for block in range(blocks):
        out_ref[block] = result


def series_kernel(
    own_ref, result_ref, inverse_ref, turned_ref, offsets_ref, series_ref
):
    blocks = result_ref.shape[0] // 8
    slots = own_ref.shape[0]
    dates = inverse_ref.shape[2]
    ones = jnp.ones((8, LANES), F32).astype(BF16)
    me = lax.axis_index("date").astype(F32)
    own = own_ref[...]
    partner = lax.broadcasted_iota(jnp.int32, (slots, blocks), 1).astype(F32)
    partner = (own[:, 0:1] == partner).astype(F32).astype(BF16)
    lane = lax.broadcasted_iota(jnp.int32, (slots, LANES), 1)
    mine = lane.astype(F32) - me == own[:, 1:2] + jnp.where(lane < CHIP, 0.0, float(CHIP))
    mine = mine & (own[:, 1:2] >= 0.0)
    for axis in range(2):
        rows = result_ref[pl.ds(axis, blocks, stride=8), :]
        value = sum(dot(partner, part) for part in parts_of(rows, 3))
        value = jnp.where(mine, value, 0.0)
        for chip in range(2):
            half = jnp.where(lane < CHIP if chip == 0 else lane >= CHIP, value, 0.0)
            half = sum(dot_nt(ones, part) for part in parts_of(half, 3))
            offsets_ref[axis, chip : chip + 1, :] = half[0:1, :]
    sums = [jnp.zeros((8, LANES), F32) for _ in range(dates)]
    per = LANES // dates
    groups = [jnp.zeros((8, LANES), F32) for _ in range(blocks // per)]
    for block in range(blocks):
        value = result_ref[block * 8 : block * 8 + 8, :]
        first = jnp.broadcast_to(value[2:3], (8, LANES))
        for date in range(dates):
            sums[date] = sums[date] + jnp.where(first == date, value, 0.0)
        groups[block // per] = groups[block // per] + value
    low = lax.broadcasted_iota(jnp.int32, (dates, LANES), 1) < CHIP
    for axis in range(2):
        own = jnp.zeros((dates, LANES), F32)
        for date in range(dates):
            own = own + turned_ref[axis, date] * sums[date][axis : axis + 1]
        for chip in range(2):
            total = jnp.where(low if chip == 0 else ~low, -own, 0.0)
            at = 4 + 2 * axis + chip
            for g, group in enumerate(groups):
                total = total + inverse_ref[axis, chip, :, g * LANES : (g + 1) * LANES] * group[at : at + 1]
            total = sum(dot_nt(ones, part) for part in parts_of(total, 3))
            series_ref[axis, chip : chip + 1, :] = total[0:1, :]


def body(images, inverse_blocks, pair_first, pair_block, pair_second, pair_count, shifts, anchors):
    blocks = lax.axis_size("date")
    strips = lax.axis_size("strip")
    dates, length, columns = images.shape
    slots = pair_first.shape[0]
    hbm = pl.BlockSpec(memory_space=pltpu.HBM)
    vmem = pl.BlockSpec(memory_space=pltpu.VMEM)
    params = pltpu.CompilerParams(vmem_limit_bytes=48 * 2**20)
    ends = strips - 1
    above = lax.ppermute(
        images[:, length - SMAX :, :], "strip", [(i, i + 1) for i in range(ends)]
    )
    below = lax.ppermute(images[:, :SMAX, :], "strip", [(i + 1, i) for i in range(ends)])
    turned = inverse_blocks.reshape(2, 2, dates, blocks, dates).transpose(0, 4, 2, 1, 3)
    turned = jnp.concatenate([turned, turned], axis=4)
    turned = jnp.pad(turned, ((0, 0),) * 4 + ((0, CHIP - 2 * blocks),))
    turned = turned.reshape(2, dates, dates, LANES)
    near_table, far_table, forward, form, across = [jnp.asarray(t) for t in make_tables()]
    send, own = pl.pallas_call(
        pack_kernel,
        out_shape=(
            jax.ShapeDtypeStruct((blocks, 2 * length + 8, columns), BF16),
            jax.ShapeDtypeStruct((slots, columns), F32),
        ),
        in_specs=[hbm] * 7 + [vmem] * 2,
        out_specs=(vmem, vmem),
        scratch_shapes=[
            pltpu.VMEM(images.shape, BF16),
            pltpu.SMEM((slots,), jnp.int32),
            pltpu.SMEM((slots,), jnp.int32),
            pltpu.SMEM((slots,), jnp.int32),
            pltpu.SMEM((1,), jnp.int32),
            pltpu.SMEM((2, 2, slots), jnp.int32),
            pltpu.SMEM((2,), jnp.int32),
            pltpu.VMEM((dates, length, columns), BF16),
            pltpu.VMEM((blocks * 8, columns), F32),
            pltpu.SMEM((blocks,), jnp.int32),
            pltpu.SMEM((slots,), jnp.int32),
            pltpu.SemaphoreType.DMA((7,)),
        ],
        compiler_params=pltpu.CompilerParams(vmem_limit_bytes=60 * 2**20),
    )(
        pair_first, pair_block[:, 0], pair_second, pair_count,
        jnp.transpose(shifts, (1, 2, 0)), anchors, images, near_table, forward,
    )
    recv = lax.all_to_all(send, "date", split_axis=0, concat_axis=0, tiled=True)
    recv, turned = lax.optimization_barrier((recv, turned))
    result = pl.pallas_call(
        match_kernel,
        out_shape=jax.ShapeDtypeStruct((blocks, 8, columns), F32),
        in_specs=[vmem] * 8,
        out_specs=vmem,
        scratch_shapes=[
            pltpu.VMEM((dates, length + 2 * SMAX, columns), F32),
            pltpu.VMEM((blocks * 8, columns), F32),
            pltpu.VMEM((8, columns), jnp.int32),
            pltpu.SMEM((8, columns), jnp.int32),
            pltpu.SMEM((CHIP + BATCH,), jnp.int32),
            pltpu.VMEM((BATCH * length, columns), BF16),
            pltpu.VMEM((BATCH * length, columns), BF16),
            pltpu.VMEM((CHIP + 8, columns), F32),
            pltpu.VMEM((CHIP + 8, columns), F32),
            pltpu.VMEM((CHIP + 8, columns), F32),
            pltpu.SemaphoreType.DMA,
        ],
        compiler_params=params,
    )(recv, images, above, below, far_table, forward, form, across)
    result = lax.all_to_all(result, "date", split_axis=0, concat_axis=0, tiled=True)
    offsets, series = pl.pallas_call(
        series_kernel,
        out_shape=(
            jax.ShapeDtypeStruct((2, 2, slots), F32),
            jax.ShapeDtypeStruct((2, 2, dates), F32),
        ),
        in_specs=[vmem] * 4,
        out_specs=(vmem, vmem),
        compiler_params=params,
    )(own, result.reshape(blocks * 8, columns), inverse_blocks, turned)
    return jnp.transpose(offsets, (2, 0, 1)), series


def solution(mesh):
    return jax.shard_map(
        body,
        mesh=mesh,
        in_specs=(
            P("date", "strip", None),
            P(None, "strip", "date", None),
            P("date"),
            P("date", None),
            P("date"),
            P("date"),
            P("date", None, "strip"),
            P("strip"),
        ),
        out_specs=(P("date", None, "strip"), P(None, "strip", "date")),
        check_vma=False,
    )
```

```python
import math

import jax
import jax.numpy as jnp
import ml_dtypes
import numpy as np
from jax import lax
from jax.experimental import pallas as pl
from jax.experimental.pallas import tpu as pltpu
from jax.sharding import PartitionSpec as P

SMAX = 8
CHIP = 64
LANES = 128
BATCH = 16
F32 = jnp.float32
BF16 = jnp.bfloat16


def make_tables():
    half = CHIP // 2
    counter = np.arange(CHIP)
    freq = counter % half
    def basis(places, length):
        turn = 2.0 * math.pi * freq[:, None] * places[None, :] / length
        value = np.where(counter[:, None] < half, np.cos(turn), np.sin(turn))
        value[half] = np.cos(2.0 * math.pi * half * places / length)
        return value
    scale = np.where(freq == 0, 1.0, math.sqrt(2.0))[:, None]
    forward = basis(counter, CHIP) * scale
    cosine, sine = forward[:half].T, forward[half:].T
    zero = np.zeros((CHIP, half))
    def spread(block):
        return np.concatenate([np.concatenate([block, zero], 1), np.concatenate([zero, block], 1)], 0)
    nyquist = cosine.copy(); nyquist[:, 0] = sine[:, 0]
    plain = sine.copy(); plain[:, 0] = 0.0
    near = np.concatenate([spread(cosine), spread(sine)], 1)
    far = np.concatenate([spread(cosine), spread(nyquist), spread(plain), spread(plain)], 1)
    places = np.arange(2 * CHIP)
    displace = ((places + CHIP) % (2 * CHIP) - CHIP) * 0.5
    wave = basis(places, 2 * CHIP)
    form = (wave * displace) @ wave.T / (2 * CHIP)
    cc, cs, sc, ss = form[:half, :half], form[:half, half:], form[half:, :half], form[half:, half:]
    two = np.eye(2)
    across = np.block([[np.kron(two, cc), np.kron(two, cs)], [np.kron(two, sc), np.kron(two, ss)]])
    tables = (near, far, forward, form, across)
    return tuple(a.astype(ml_dtypes.bfloat16) for a in tables)


def dot(a, b):
    return lax.dot_general(a, b, (((1,), (0,)), ((), ())), preferred_element_type=F32)


def dot_nt(a, b):
    return lax.dot_general(a, b, (((1,), (1,)), ((), ())), preferred_element_type=F32)


def parts_of(value, count):
    parts = []
    for _ in range(count):
        part = value.astype(BF16)
        parts.append(part)
        value = value - part.astype(F32)
    return parts


def level_lanes():
    lane = lax.broadcasted_iota(jnp.int32, (1, LANES), 1)
    return jnp.where((lane < CHIP) & (lane % (CHIP // 2) == 0), 1.0 / CHIP, 0.0)


def pack_kernel(
    first_hbm, block_hbm, second_hbm, count_hbm, shifts_hbm, anchors_hbm, images_hbm,
    table_ref, forward_ref,
    send_ref, own_ref, images_ref,
    first_ref, block_ref, second_ref, count_ref, shifts_ref, anchors_ref,
    near_ref, facts_ref, tally_ref, where_ref, sems,
):
    dates = images_ref.shape[0]
    blocks = send_ref.shape[0]
    slots = first_ref.shape[0]
    copies = [
        pltpu.make_async_copy(source, target, sems.at[index])
        for index, (source, target) in enumerate(
            (
                (anchors_hbm, anchors_ref), (first_hbm, first_ref), (block_hbm, block_ref),
                (second_hbm, second_ref), (count_hbm, count_ref), (shifts_hbm, shifts_ref),
                (images_hbm, images_ref),
            )
        )
    ]
    for copy in copies:
        copy.start()
    facts_ref[...] = jnp.zeros(facts_ref.shape, F32)
    for block in range(blocks):
        tally_ref[block] = 0
    for copy in copies[:-1]:
        copy.wait()
    place = lax.broadcasted_iota(jnp.int32, (1, LANES), 1)
    for slot in range(slots):
        block = block_ref[slot]
        rank = tally_ref[block]
        tally_ref[block] = rank + 1
        where_ref[slot] = rank
        live = jnp.where(slot < count_ref[0], 1, 0)
        values = [live, second_ref[slot]]
        for chip in range(2):
            start = shifts_ref[1, chip, slot] + anchors_ref[chip] - chip * CHIP
            values += [shifts_ref[0, chip, slot], start]
        values += [first_ref[slot], shifts_ref[1, 0, slot], shifts_ref[1, 1, slot]]
        fact = jnp.zeros((1, LANES), jnp.int32)
        for index, value in enumerate(values):
            fact = jnp.where(place == index, value, fact)
        facts_ref[pl.ds(block * 8 + rank, 1), :] = fact.astype(F32)
        own = jnp.where(place == 0, block, jnp.where(live > 0, rank * blocks, -1))
        own_ref[slot : slot + 1, :] = own.astype(F32)
    row = lax.broadcasted_iota(jnp.int32, (LANES, LANES), 0)
    lane = lax.broadcasted_iota(jnp.int32, (LANES, LANES), 1)
    column = lane + jnp.where(lane < CHIP, anchors_ref[0], anchors_ref[1] - CHIP)
    pick = (row == column).astype(F32).astype(BF16)
    table = dot(pick, table_ref[...]).astype(BF16)
    level = level_lanes()
    copies[-1].wait()
    section = dot(images_ref[...].reshape(dates * CHIP, LANES), table)
    parts = []
    for date in range(dates):
        part = section[date * CHIP : (date + 1) * CHIP]
        parts.append((part - level * jnp.sum(part, axis=0, keepdims=True)).astype(BF16))
    for date in range(0, dates, 2):
        pair = dot(forward_ref[...], jnp.concatenate(parts[date : date + 2], axis=1)).astype(BF16)
        near_ref[date] = pair[:, :LANES]
        near_ref[date + 1] = pair[:, LANES:]
    for slot in range(slots):
        at = pl.multiple_of(where_ref[slot] * CHIP, CHIP)
        send_ref[block_ref[slot], pl.ds(at, CHIP), :] = near_ref[first_ref[slot]]
    send_ref[:, 2 * CHIP : 2 * CHIP + 8, :] = (
        facts_ref[...].reshape(blocks, 8, LANES).astype(BF16)
    )


def match_kernel(
    recv_ref, images_ref, above_ref, below_ref,
    table_ref, forward_ref, form_ref, across_ref, out_ref,
    framed_ref, facts_ref, whole_ref, scalar_ref, list_ref, data_ref, cross_ref,
    energy_ref, tall_ref, wide_ref, copy_sem,
):
    blocks = recv_ref.shape[0]
    dates = images_ref.shape[0]
    half = CHIP // 2
    facts_ref[...] = recv_ref[:, 2 * CHIP : 2 * CHIP + 8, :].astype(F32).reshape(blocks * 8, LANES)
    whole = [facts_ref[pl.ds(rank, blocks, stride=8), :].astype(BF16) for rank in range(2)]
    if blocks < CHIP // 2:
        whole.append(jnp.zeros((CHIP - 2 * blocks, LANES), BF16))
    lane16 = lax.broadcasted_iota(jnp.int32, (16, LANES), 1)
    row16 = lax.broadcasted_iota(jnp.int32, (16, LANES), 0)
    choose = (lane16 == row16).astype(F32).astype(BF16)
    fact = dot_nt(choose, jnp.concatenate(whole + whole, axis=0))
    whole_ref[...] = fact[:8].astype(jnp.int32)
    copy = pltpu.make_async_copy(whole_ref, scalar_ref, copy_sem)
    copy.start()
    framed_ref[:, :SMAX, :] = above_ref[...].astype(F32)
    framed_ref[:, SMAX : SMAX + CHIP, :] = images_ref[...].astype(F32)
    framed_ref[:, SMAX + CHIP :, :] = below_ref[...].astype(F32)
    for ref in (energy_ref, tall_ref, wide_ref):
        ref[...] = jnp.zeros(ref.shape, F32)
    copy.wait()

    count = 0
    for slot in range(2 * blocks):
        list_ref[count] = slot
        count = count + scalar_ref[0, slot]
    spare = CHIP
    for extra in range(BATCH):
        list_ref[count + extra] = spare
    lane = lax.broadcasted_iota(jnp.int32, (1, LANES), 1)
    low = lane < CHIP
    level = level_lanes()
    turn_sign = jnp.where(lane % half == 0, 0.0, jnp.where(low, 1.0, -1.0))
    corner = jnp.where((lane % half == 0) & (lane >= CHIP), 1.0, 0.0)
    top_row = lax.broadcasted_iota(jnp.int32, (8, LANES), 0) == 0

    def one_batch(turn, carry):
        rows_of = []
        near_of = []
        for s in range(BATCH):
            slot = list_ref[turn * BATCH + s]
            rows_of.append(slot)
            source = jnp.where(slot == spare, 0, slot)
            rank = jnp.where(source >= blocks, 1, 0)
            near_of.append((source - rank * blocks, pl.multiple_of(rank * CHIP, CHIP)))
            second = scalar_ref[1, source]
            pieces = []
            starts = []
            for chip in range(2):
                down = scalar_ref[2 + 2 * chip, source] + SMAX
                start = scalar_ref[3 + 2 * chip, source]
                piece = framed_ref[second, pl.ds(down, CHIP), :]
                pieces.append(pltpu.roll(piece, lax.rem(LANES - start, LANES), 1))
                starts.append(start)
            column = lane + jnp.where(low, starts[0], starts[1])
            inside = (column >= 0) & (column < LANES)
            window = jnp.where(low, pieces[0], pieces[1])
            data_ref[s * CHIP : (s + 1) * CHIP, :] = jnp.where(inside, window, 0.0).astype(BF16)
        section = dot(data_ref[...], table_ref[...])
        crosses = []
        for s in range(BATCH):
            part = section[s * CHIP : (s + 1) * CHIP, :LANES]
            part = part - level * jnp.sum(part, axis=0, keepdims=True)
            other = section[s * CHIP : (s + 1) * CHIP, LANES:]
            far = dot(forward_ref[...], jnp.concatenate([part, other], axis=1).astype(BF16))
            block, at = near_of[s]
            near = recv_ref[block, pl.ds(at, CHIP), :].astype(F32)
            turned = pltpu.roll(near, CHIP, 1) * turn_sign
            top, low_rows = near[:half], near[half:]
            top_turned, low_turned = turned[:half], turned[half:]
            p, q = far[:half, :LANES], far[:half, LANES:]
            p_low, q_low = far[half:, :LANES], far[half:, LANES:]
            first = top * p + top_turned * q
            second = low_rows * p_low + low_turned * q_low
            upper = first + second
            lower = (low_rows * p + low_turned * q) - (top * p_low + top_turned * q_low)
            upper = jnp.concatenate([jnp.where(top_row, first[:8], upper[:8]), upper[8:]], axis=0)
            lower = jnp.concatenate([jnp.where(top_row, second[:8], lower[:8]), lower[8:]], axis=0)
            cross = jnp.concatenate([upper, lower], axis=0)
            crosses.append(cross)
            cross_ref[s * CHIP : (s + 1) * CHIP, :] = cross.astype(BF16)
        wide = dot(cross_ref[...], across_ref[...])
        for s in range(0, BATCH, 2):
            pair = [cross_ref[r * CHIP : (r + 1) * CHIP, :] for r in (s, s + 1)]
            tall = dot(form_ref[...], jnp.concatenate(pair, axis=1))
            for r in range(2):
                cross = crosses[s + r]
                power = cross * cross
                tall_r = cross * tall[:, r * LANES : (r + 1) * LANES]
                wide_r = cross * wide[(s + r) * CHIP : (s + r + 1) * CHIP]
                at = pl.ds(rows_of[s + r], 1)
                energy_ref[at, :] = 0.5 * (
                    jnp.sum(power, axis=0, keepdims=True)
                    + power[:1] + corner * power[half : half + 1]
                )
                tall_ref[at, :] = jnp.sum(tall_r, axis=0, keepdims=True)
                wide_ref[at, :] = 0.5 * (jnp.sum(wide_r, axis=0, keepdims=True) + wide_r[:1])
        return carry

    lax.fori_loop(0, (count + BATCH - 1) // BATCH, one_batch, 0)

    lane8 = lax.broadcasted_iota(jnp.int32, (8, LANES), 1)
    row8 = lax.broadcasted_iota(jnp.int32, (8, LANES), 0)
    weights = jnp.where((row8 == 1) | ((lane8 % half == 0) & (lane8 < CHIP)), 1.0, 0.5)
    even = lane // half % 2 == 0
    stack = []
    for ref in (energy_ref, tall_ref, wide_ref):
        value = ref[:CHIP, :]
        stack += [jnp.where(even, value, 0.0), jnp.where(even, 0.0, value)]
    weights = weights.astype(BF16)
    found = sum(dot_nt(weights, part) for part in parts_of(jnp.concatenate(stack, axis=0), 3))
    norm = found[0:1, :LANES] + 1e-6
    tall = found[0:1, LANES : 2 * LANES] / norm
    wide = found[1:2, 2 * LANES :] / norm
    live = fact[0:1] > 0.5
    down = jnp.where(live, jnp.where(low, fact[2:3], fact[4:5]) + tall, 0.0)
    across = jnp.where(live, jnp.where(low, fact[7:8], fact[8:9]) + wide, 0.0)
    row = lax.broadcasted_iota(jnp.int32, (LANES, LANES), 0)
    row = jnp.where(row < CHIP, -1, row % dates).astype(F32)
    chosen = (row == fact[1:2]).astype(F32).astype(BF16)
    value = jnp.where(row8 < 2, down, across)
    value = jnp.where((row8 < 4) & ((row8 % 2 == 0) == (lane8 < CHIP)), value, 0.0)
    sums = dot_nt(jnp.concatenate(parts_of(value, 3), axis=0), chosen)
    sums = sums[:8] + sums[8:16] + sums[16:24]
    sums = jnp.where((lane8 - CHIP) // dates == row8, sums, 0.0)
    sums = jnp.sum(sums, axis=0, keepdims=True)
    sums = jnp.where(low, fact[6:7], sums)
    result = jnp.where(row8 == 0, down, jnp.where(row8 == 1, across, sums))
    for block in range(blocks):
        out_ref[block] = result[:4]


def series_kernel(
    own_ref, result_ref, firsts_ref, seconds_ref, offsets_ref, series_ref
):
    blocks = result_ref.shape[0] // 4
    slots = own_ref.shape[0]
    dates = seconds_ref.shape[0]
    me = lax.axis_index("date").astype(F32)
    own = own_ref[...]
    partner = lax.broadcasted_iota(jnp.int32, (slots, blocks), 1).astype(F32)
    partner = (own[:, 0:1] == partner).astype(F32).astype(BF16)
    lane = lax.broadcasted_iota(jnp.int32, (slots, LANES), 1)
    mine = lane.astype(F32) - me == own[:, 1:2] + jnp.where(lane < CHIP, 0.0, float(CHIP))
    mine = mine & (own[:, 1:2] >= 0.0)
    facts = result_ref[pl.ds(2, blocks, stride=4), :]
    low = lax.broadcasted_iota(jnp.int32, (blocks, LANES), 1) < CHIP
    first = jnp.where(low, facts, pltpu.roll(facts, CHIP, 1))
    lane8 = lax.broadcasted_iota(jnp.int32, (8, LANES), 1)
    row8 = lax.broadcasted_iota(jnp.int32, (8, LANES), 0)
    chips = (lane8 // CHIP == row8).astype(F32).astype(BF16)
    pieces = ((lane8 - CHIP) // dates == row8).astype(F32).astype(BF16)
    total = jnp.concatenate(
        [jnp.sum(seconds_ref[date] * facts, axis=0, keepdims=True) for date in range(dates)],
        axis=0,
    )
    gained = sum(dot_nt(pieces, part) for part in parts_of(total, 3))
    for axis in range(2):
        rows = result_ref[pl.ds(axis, blocks, stride=4), :]
        value = sum(dot(partner, part) for part in parts_of(rows, 3))
        value = jnp.where(mine, value, 0.0)
        value = sum(dot_nt(chips, part) for part in parts_of(value, 3))
        offsets_ref[axis] = value[:2]
        total = jnp.zeros((dates, LANES), F32)
        for date in range(dates):
            here = jnp.sum(jnp.where(first == date, rows, 0.0), axis=0, keepdims=True)
            total = total + firsts_ref[axis, date] * here
        lost = sum(dot_nt(chips, part) for part in parts_of(total, 3))
        series_ref[axis] = gained[2 * axis : 2 * axis + 2] - lost[:2]


def body(images, inverse_blocks, pair_first, pair_block, pair_second, pair_count, shifts, anchors):
    blocks = lax.axis_size("date")
    strips = lax.axis_size("strip")
    dates, length, columns = images.shape
    slots = pair_first.shape[0]
    hbm = pl.BlockSpec(memory_space=pltpu.HBM)
    vmem = pl.BlockSpec(memory_space=pltpu.VMEM)
    params = pltpu.CompilerParams(vmem_limit_bytes=48 * 2**20)
    ends = strips - 1
    above = lax.ppermute(
        images[:, length - SMAX :, :], "strip", [(i, i + 1) for i in range(ends)]
    )
    below = lax.ppermute(images[:, :SMAX, :], "strip", [(i + 1, i) for i in range(ends)])
    turned = inverse_blocks.reshape(2, 2, dates, blocks, dates).transpose(0, 4, 2, 1, 3)
    turned = jnp.concatenate([turned, turned], axis=4)
    turned = jnp.pad(turned, ((0, 0),) * 4 + ((0, CHIP - 2 * blocks),))
    firsts = turned.reshape(2, dates, dates, LANES)
    seconds = inverse_blocks.reshape(2, 2, dates, blocks, dates).transpose(2, 3, 0, 1, 4)
    seconds = jnp.pad(seconds.reshape(dates, blocks, 4 * dates), ((0, 0), (0, 0), (CHIP, 0)))
    near_table, far_table, forward, form, across = [jnp.asarray(t) for t in make_tables()]
    send, own = pl.pallas_call(
        pack_kernel,
        out_shape=(
            jax.ShapeDtypeStruct((blocks, 2 * length + 8, columns), BF16),
            jax.ShapeDtypeStruct((slots, columns), F32),
        ),
        in_specs=[hbm] * 7 + [vmem] * 2,
        out_specs=(vmem, vmem),
        scratch_shapes=[
            pltpu.VMEM(images.shape, BF16),
            pltpu.SMEM((slots,), jnp.int32),
            pltpu.SMEM((slots,), jnp.int32),
            pltpu.SMEM((slots,), jnp.int32),
            pltpu.SMEM((1,), jnp.int32),
            pltpu.SMEM((2, 2, slots), jnp.int32),
            pltpu.SMEM((2,), jnp.int32),
            pltpu.VMEM((dates, length, columns), BF16),
            pltpu.VMEM((blocks * 8, columns), F32),
            pltpu.SMEM((blocks,), jnp.int32),
            pltpu.SMEM((slots,), jnp.int32),
            pltpu.SemaphoreType.DMA((7,)),
        ],
        compiler_params=pltpu.CompilerParams(vmem_limit_bytes=60 * 2**20),
    )(
        pair_first, pair_block[:, 0], pair_second, pair_count,
        jnp.transpose(shifts, (1, 2, 0)), anchors, images, near_table, forward,
    )
    recv = lax.all_to_all(send, "date", split_axis=0, concat_axis=0, tiled=True)
    recv, firsts, seconds = lax.optimization_barrier((recv, firsts, seconds))
    result = pl.pallas_call(
        match_kernel,
        out_shape=jax.ShapeDtypeStruct((blocks, 4, columns), F32),
        in_specs=[vmem] * 8,
        out_specs=vmem,
        scratch_shapes=[
            pltpu.VMEM((dates, length + 2 * SMAX, columns), F32),
            pltpu.VMEM((blocks * 8, columns), F32),
            pltpu.VMEM((8, columns), jnp.int32),
            pltpu.SMEM((8, columns), jnp.int32),
            pltpu.SMEM((CHIP + BATCH,), jnp.int32),
            pltpu.VMEM((BATCH * length, columns), BF16),
            pltpu.VMEM((BATCH * length, columns), BF16),
            pltpu.VMEM((CHIP + 8, columns), F32),
            pltpu.VMEM((CHIP + 8, columns), F32),
            pltpu.VMEM((CHIP + 8, columns), F32),
            pltpu.SemaphoreType.DMA,
        ],
        compiler_params=params,
    )(recv, images, above, below, far_table, forward, form, across)
    result = lax.all_to_all(result, "date", split_axis=0, concat_axis=0, tiled=True)
    offsets, series = pl.pallas_call(
        series_kernel,
        out_shape=(
            jax.ShapeDtypeStruct((2, 2, slots), F32),
            jax.ShapeDtypeStruct((2, 2, dates), F32),
        ),
        in_specs=[vmem] * 4,
        out_specs=(vmem, vmem),
        compiler_params=params,
    )(own, result.reshape(blocks * 4, columns), firsts, seconds)
    return jnp.transpose(offsets, (2, 0, 1)), series


def solution(mesh):
    return jax.shard_map(
        body,
        mesh=mesh,
        in_specs=(
            P("date", "strip", None),
            P(None, "strip", "date", None),
            P("date"),
            P("date", None),
            P("date"),
            P("date"),
            P("date", None, "strip"),
            P("strip"),
        ),
        out_specs=(P("date", None, "strip"), P(None, "strip", "date")),
        check_vma=False,
    )
```

```python
import math

import jax
import jax.numpy as jnp
import ml_dtypes
import numpy as np
from jax import lax
from jax.experimental import pallas as pl
from jax.experimental.pallas import tpu as pltpu
from jax.sharding import PartitionSpec as P

SMAX = 8
CHIP = 64
LANES = 128
BATCH = 32
F32 = jnp.float32
BF16 = jnp.bfloat16


def make_tables():
    half = CHIP // 2
    counter = np.arange(CHIP)
    freq = counter % half
    def basis(places, length):
        turn = 2.0 * math.pi * freq[:, None] * places[None, :] / length
        value = np.where(counter[:, None] < half, np.cos(turn), np.sin(turn))
        value[half] = np.cos(2.0 * math.pi * half * places / length)
        return value
    scale = np.where(freq == 0, 1.0, math.sqrt(2.0))[:, None]
    forward = basis(counter, CHIP) * scale
    cosine, sine = forward[:half].T, forward[half:].T
    zero = np.zeros((CHIP, half))
    def spread(block):
        return np.concatenate([np.concatenate([block, zero], 1), np.concatenate([zero, block], 1)], 0)
    nyquist = cosine.copy(); nyquist[:, 0] = sine[:, 0]
    plain = sine.copy(); plain[:, 0] = 0.0
    near = np.concatenate([spread(cosine), spread(sine)], 1)
    far = np.concatenate([spread(cosine), spread(nyquist), spread(plain), spread(plain)], 1)
    places = np.arange(2 * CHIP)
    displace = ((places + CHIP) % (2 * CHIP) - CHIP) * 0.5
    wave = basis(places, 2 * CHIP)
    form = (wave * displace) @ wave.T / (2 * CHIP)
    cc, cs, sc, ss = form[:half, :half], form[:half, half:], form[half:, :half], form[half:, half:]
    two = np.eye(2)
    across = np.block([[np.kron(two, cc), np.kron(two, cs)], [np.kron(two, sc), np.kron(two, ss)]])
    tables = (near, far, forward, form, across)
    return tuple(a.astype(ml_dtypes.bfloat16) for a in tables)


def dot(a, b):
    return lax.dot_general(a, b, (((1,), (0,)), ((), ())), preferred_element_type=F32)


def dot_nt(a, b):
    return lax.dot_general(a, b, (((1,), (1,)), ((), ())), preferred_element_type=F32)


def parts_of(value, count):
    parts = []
    for _ in range(count):
        part = value.astype(BF16)
        parts.append(part)
        value = value - part.astype(F32)
    return parts


def level_lanes():
    lane = lax.broadcasted_iota(jnp.int32, (1, LANES), 1)
    return jnp.where((lane < CHIP) & (lane % (CHIP // 2) == 0), 1.0 / CHIP, 0.0)


def pack_kernel(
    first_hbm, block_hbm, second_hbm, count_hbm, shifts_hbm, anchors_hbm, images_hbm,
    table_hbm, forward_hbm,
    send_ref, own_ref, images_ref, table_ref, forward_ref,
    first_ref, block_ref, second_ref, count_ref, shifts_ref, anchors_ref,
    near_ref, facts_ref, tally_ref, where_ref, sems,
):
    dates = images_ref.shape[0]
    blocks = send_ref.shape[0]
    slots = first_ref.shape[0]
    copies = [
        pltpu.make_async_copy(source, target, sems.at[index])
        for index, (source, target) in enumerate(
            (
                (anchors_hbm, anchors_ref), (first_hbm, first_ref), (block_hbm, block_ref),
                (second_hbm, second_ref), (count_hbm, count_ref), (shifts_hbm, shifts_ref),
                (table_hbm, table_ref), (forward_hbm, forward_ref), (images_hbm, images_ref),
            )
        )
    ]
    for copy in copies:
        copy.start()
    facts_ref[...] = jnp.zeros(facts_ref.shape, F32)
    for block in range(blocks):
        tally_ref[block] = 0
    for copy in copies[:6]:
        copy.wait()
    place = lax.broadcasted_iota(jnp.int32, (1, LANES), 1)
    for slot in range(slots):
        block = block_ref[slot]
        rank = tally_ref[block]
        tally_ref[block] = rank + 1
        where_ref[slot] = rank
        live = jnp.where(slot < count_ref[0], 1, 0)
        values = [live, second_ref[slot]]
        for chip in range(2):
            start = shifts_ref[1, chip, slot] + anchors_ref[chip] - chip * CHIP
            values += [shifts_ref[0, chip, slot], start]
        values += [first_ref[slot], shifts_ref[1, 0, slot], shifts_ref[1, 1, slot]]
        fact = jnp.zeros((1, LANES), jnp.int32)
        for index, value in enumerate(values):
            fact = jnp.where(place == index, value, fact)
        facts_ref[pl.ds(block * 8 + rank, 1), :] = fact.astype(F32)
        own = jnp.where(place == 0, block, jnp.where(live > 0, rank * blocks, -1))
        own_ref[slot : slot + 1, :] = own.astype(F32)
    row = lax.broadcasted_iota(jnp.int32, (LANES, LANES), 0)
    lane = lax.broadcasted_iota(jnp.int32, (LANES, LANES), 1)
    column = lane + jnp.where(lane < CHIP, anchors_ref[0], anchors_ref[1] - CHIP)
    pick = (row == column).astype(F32).astype(BF16)
    for copy in copies[6:8]:
        copy.wait()
    table = dot(pick, table_ref[...]).astype(BF16)
    level = level_lanes()
    copies[-1].wait()
    section = dot(images_ref[...].reshape(dates * CHIP, LANES), table)
    parts = []
    for date in range(dates):
        part = section[date * CHIP : (date + 1) * CHIP]
        parts.append((part - level * jnp.sum(part, axis=0, keepdims=True)).astype(BF16))
    for date in range(0, dates, 2):
        pair = dot(forward_ref[...], jnp.concatenate(parts[date : date + 2], axis=1)).astype(BF16)
        near_ref[date] = pair[:, :LANES]
        near_ref[date + 1] = pair[:, LANES:]
    for slot in range(slots):
        at = pl.multiple_of(where_ref[slot] * CHIP, CHIP)
        send_ref[block_ref[slot], pl.ds(at, CHIP), :] = near_ref[first_ref[slot]]
    send_ref[:, 2 * CHIP : 2 * CHIP + 8, :] = (
        facts_ref[...].reshape(blocks, 8, LANES).astype(BF16)
    )


def match_kernel(
    recv_ref, images_ref, above_ref, below_ref,
    table_ref, forward_ref, form_ref, across_ref, out_ref,
    framed_ref, facts_ref, whole_ref, scalar_ref, list_ref, data_ref, cross_ref,
    energy_ref, tall_ref, wide_ref, copy_sem,
):
    blocks = recv_ref.shape[0]
    dates = images_ref.shape[0]
    half = CHIP // 2
    facts_ref[...] = recv_ref[:, 2 * CHIP : 2 * CHIP + 8, :].astype(F32).reshape(blocks * 8, LANES)
    whole = [facts_ref[pl.ds(rank, blocks, stride=8), :].astype(BF16) for rank in range(2)]
    if blocks < CHIP // 2:
        whole.append(jnp.zeros((CHIP - 2 * blocks, LANES), BF16))
    lane16 = lax.broadcasted_iota(jnp.int32, (16, LANES), 1)
    row16 = lax.broadcasted_iota(jnp.int32, (16, LANES), 0)
    choose = (lane16 == row16).astype(F32).astype(BF16)
    fact = dot_nt(choose, jnp.concatenate(whole + whole, axis=0))
    whole_ref[...] = fact[:8].astype(jnp.int32)
    copy = pltpu.make_async_copy(whole_ref, scalar_ref, copy_sem)
    copy.start()
    framed_ref[:, :SMAX, :] = above_ref[...].astype(F32)
    framed_ref[:, SMAX : SMAX + CHIP, :] = images_ref[...].astype(F32)
    framed_ref[:, SMAX + CHIP :, :] = below_ref[...].astype(F32)
    for ref in (energy_ref, tall_ref, wide_ref):
        ref[...] = jnp.zeros(ref.shape, F32)
    copy.wait()

    count = 0
    for slot in range(2 * blocks):
        list_ref[count] = slot
        count = count + scalar_ref[0, slot]
    spare = CHIP
    for extra in range(BATCH):
        list_ref[count + extra] = spare
    lane = lax.broadcasted_iota(jnp.int32, (1, LANES), 1)
    low = lane < CHIP
    level = level_lanes()
    turn_sign = jnp.where(lane % half == 0, 0.0, jnp.where(low, 1.0, -1.0))
    corner = jnp.where((lane % half == 0) & (lane >= CHIP), 1.0, 0.0)
    top_row = lax.broadcasted_iota(jnp.int32, (8, LANES), 0) == 0

    def one_batch(turn, carry):
        rows_of = []
        near_of = []
        for s in range(BATCH):
            slot = list_ref[turn * BATCH + s]
            rows_of.append(slot)
            source = jnp.where(slot == spare, 0, slot)
            rank = jnp.where(source >= blocks, 1, 0)
            near_of.append((source - rank * blocks, pl.multiple_of(rank * CHIP, CHIP)))
            second = scalar_ref[1, source]
            pieces = []
            starts = []
            for chip in range(2):
                down = scalar_ref[2 + 2 * chip, source] + SMAX
                start = scalar_ref[3 + 2 * chip, source]
                piece = framed_ref[second, pl.ds(down, CHIP), :]
                pieces.append(pltpu.roll(piece, lax.rem(LANES - start, LANES), 1))
                starts.append(start)
            column = lane + jnp.where(low, starts[0], starts[1])
            inside = (column >= 0) & (column < LANES)
            window = jnp.where(low, pieces[0], pieces[1])
            data_ref[s * CHIP : (s + 1) * CHIP, :] = jnp.where(inside, window, 0.0).astype(BF16)
        section = dot(data_ref[...], table_ref[...])
        crosses = []
        for s in range(BATCH):
            part = section[s * CHIP : (s + 1) * CHIP, :LANES]
            part = part - level * jnp.sum(part, axis=0, keepdims=True)
            other = section[s * CHIP : (s + 1) * CHIP, LANES:]
            far = dot(forward_ref[...], jnp.concatenate([part, other], axis=1).astype(BF16))
            block, at = near_of[s]
            near = recv_ref[block, pl.ds(at, CHIP), :].astype(F32)
            turned = pltpu.roll(near, CHIP, 1) * turn_sign
            top, low_rows = near[:half], near[half:]
            top_turned, low_turned = turned[:half], turned[half:]
            p, q = far[:half, :LANES], far[:half, LANES:]
            p_low, q_low = far[half:, :LANES], far[half:, LANES:]
            first = top * p + top_turned * q
            second = low_rows * p_low + low_turned * q_low
            upper = first + second
            lower = (low_rows * p + low_turned * q) - (top * p_low + top_turned * q_low)
            upper = jnp.concatenate([jnp.where(top_row, first[:8], upper[:8]), upper[8:]], axis=0)
            lower = jnp.concatenate([jnp.where(top_row, second[:8], lower[:8]), lower[8:]], axis=0)
            cross = jnp.concatenate([upper, lower], axis=0)
            crosses.append(cross)
            cross_ref[s * CHIP : (s + 1) * CHIP, :] = cross.astype(BF16)
        wide = dot(cross_ref[...], across_ref[...])
        for s in range(0, BATCH, 2):
            pair = [cross_ref[r * CHIP : (r + 1) * CHIP, :] for r in (s, s + 1)]
            tall = dot(form_ref[...], jnp.concatenate(pair, axis=1))
            for r in range(2):
                cross = crosses[s + r]
                power = cross * cross
                tall_r = cross * tall[:, r * LANES : (r + 1) * LANES]
                wide_r = cross * wide[(s + r) * CHIP : (s + r + 1) * CHIP]
                at = pl.ds(rows_of[s + r], 1)
                energy_ref[at, :] = 0.5 * (
                    jnp.sum(power, axis=0, keepdims=True)
                    + power[:1] + corner * power[half : half + 1]
                )
                tall_ref[at, :] = jnp.sum(tall_r, axis=0, keepdims=True)
                wide_ref[at, :] = 0.5 * (jnp.sum(wide_r, axis=0, keepdims=True) + wide_r[:1])
        return carry

    lax.fori_loop(0, (count + BATCH - 1) // BATCH, one_batch, 0)

    lane8 = lax.broadcasted_iota(jnp.int32, (8, LANES), 1)
    row8 = lax.broadcasted_iota(jnp.int32, (8, LANES), 0)
    weights = jnp.where((row8 == 1) | ((lane8 % half == 0) & (lane8 < CHIP)), 1.0, 0.5)
    even = lane // half % 2 == 0
    stack = []
    for ref in (energy_ref, tall_ref, wide_ref):
        value = ref[:CHIP, :]
        stack += [jnp.where(even, value, 0.0), jnp.where(even, 0.0, value)]
    weights = weights.astype(BF16)
    found = sum(dot_nt(weights, part) for part in parts_of(jnp.concatenate(stack, axis=0), 3))
    norm = found[0:1, :LANES] + 1e-6
    tall = found[0:1, LANES : 2 * LANES] / norm
    wide = found[1:2, 2 * LANES :] / norm
    live = fact[0:1] > 0.5
    down = jnp.where(live, jnp.where(low, fact[2:3], fact[4:5]) + tall, 0.0)
    across = jnp.where(live, jnp.where(low, fact[7:8], fact[8:9]) + wide, 0.0)
    row = lax.broadcasted_iota(jnp.int32, (LANES, LANES), 0)
    row = jnp.where(row < CHIP, -1, row % dates).astype(F32)
    chosen = (row == fact[1:2]).astype(F32).astype(BF16)
    value = jnp.where(row8 < 2, down, across)
    value = jnp.where((row8 < 4) & ((row8 % 2 == 0) == (lane8 < CHIP)), value, 0.0)
    sums = dot_nt(jnp.concatenate(parts_of(value, 3), axis=0), chosen)
    sums = sums[:8] + sums[8:16] + sums[16:24]
    sums = jnp.where((lane8 - CHIP) // dates == row8, sums, 0.0)
    sums = jnp.sum(sums, axis=0, keepdims=True)
    sums = jnp.where(low, fact[6:7], sums)
    result = jnp.where(row8 == 0, down, jnp.where(row8 == 1, across, sums))
    for block in range(blocks):
        out_ref[block] = result[:4]


def series_kernel(
    own_ref, result_ref, firsts_ref, seconds_ref, offsets_ref, series_ref
):
    blocks = result_ref.shape[0] // 4
    slots = own_ref.shape[0]
    dates = seconds_ref.shape[0]
    me = lax.axis_index("date").astype(F32)
    own = own_ref[...]
    partner = lax.broadcasted_iota(jnp.int32, (slots, blocks), 1).astype(F32)
    partner = (own[:, 0:1] == partner).astype(F32).astype(BF16)
    lane = lax.broadcasted_iota(jnp.int32, (slots, LANES), 1)
    mine = lane.astype(F32) - me == own[:, 1:2] + jnp.where(lane < CHIP, 0.0, float(CHIP))
    mine = mine & (own[:, 1:2] >= 0.0)
    facts = result_ref[pl.ds(2, blocks, stride=4), :]
    low = lax.broadcasted_iota(jnp.int32, (blocks, LANES), 1) < CHIP
    first = jnp.where(low, facts, pltpu.roll(facts, CHIP, 1))
    lane8 = lax.broadcasted_iota(jnp.int32, (8, LANES), 1)
    row8 = lax.broadcasted_iota(jnp.int32, (8, LANES), 0)
    chips = (lane8 // CHIP == row8).astype(F32).astype(BF16)
    pieces = ((lane8 - CHIP) // dates == row8).astype(F32).astype(BF16)
    total = jnp.concatenate(
        [jnp.sum(seconds_ref[date] * facts, axis=0, keepdims=True) for date in range(dates)],
        axis=0,
    )
    gained = sum(dot_nt(pieces, part) for part in parts_of(total, 3))
    for axis in range(2):
        rows = result_ref[pl.ds(axis, blocks, stride=4), :]
        value = sum(dot(partner, part) for part in parts_of(rows, 3))
        value = jnp.where(mine, value, 0.0)
        value = sum(dot_nt(chips, part) for part in parts_of(value, 3))
        offsets_ref[axis] = value[:2]
        total = jnp.zeros((dates, LANES), F32)
        for date in range(dates):
            here = jnp.sum(jnp.where(first == date, rows, 0.0), axis=0, keepdims=True)
            total = total + firsts_ref[axis, date] * here
        lost = sum(dot_nt(chips, part) for part in parts_of(total, 3))
        series_ref[axis] = gained[2 * axis : 2 * axis + 2] - lost[:2]


def body(images, inverse_blocks, pair_first, pair_block, pair_second, pair_count, shifts, anchors):
    blocks = lax.axis_size("date")
    strips = lax.axis_size("strip")
    dates, length, columns = images.shape
    slots = pair_first.shape[0]
    hbm = pl.BlockSpec(memory_space=pltpu.HBM)
    vmem = pl.BlockSpec(memory_space=pltpu.VMEM)
    params = pltpu.CompilerParams(vmem_limit_bytes=48 * 2**20)
    ends = strips - 1
    above = lax.ppermute(
        images[:, length - SMAX :, :], "strip", [(i, i + 1) for i in range(ends)]
    )
    below = lax.ppermute(images[:, :SMAX, :], "strip", [(i + 1, i) for i in range(ends)])
    turned = inverse_blocks.reshape(2, 2, dates, blocks, dates).transpose(0, 4, 2, 1, 3)
    turned = jnp.concatenate([turned, turned], axis=4)
    turned = jnp.pad(turned, ((0, 0),) * 4 + ((0, CHIP - 2 * blocks),))
    firsts = turned.reshape(2, dates, dates, LANES)
    seconds = inverse_blocks.reshape(2, 2, dates, blocks, dates).transpose(2, 3, 0, 1, 4)
    seconds = jnp.pad(seconds.reshape(dates, blocks, 4 * dates), ((0, 0), (0, 0), (CHIP, 0)))
    near_table, far_table, forward, form, across = [jnp.asarray(t) for t in make_tables()]
    send, own = pl.pallas_call(
        pack_kernel,
        out_shape=(
            jax.ShapeDtypeStruct((blocks, 2 * length + 8, columns), BF16),
            jax.ShapeDtypeStruct((slots, columns), F32),
        ),
        in_specs=[hbm] * 9,
        out_specs=(vmem, vmem),
        scratch_shapes=[
            pltpu.VMEM(images.shape, BF16),
            pltpu.VMEM(near_table.shape, BF16),
            pltpu.VMEM(forward.shape, BF16),
            pltpu.SMEM((slots,), jnp.int32),
            pltpu.SMEM((slots,), jnp.int32),
            pltpu.SMEM((slots,), jnp.int32),
            pltpu.SMEM((1,), jnp.int32),
            pltpu.SMEM((2, 2, slots), jnp.int32),
            pltpu.SMEM((2,), jnp.int32),
            pltpu.VMEM((dates, length, columns), BF16),
            pltpu.VMEM((blocks * 8, columns), F32),
            pltpu.SMEM((blocks,), jnp.int32),
            pltpu.SMEM((slots,), jnp.int32),
            pltpu.SemaphoreType.DMA((9,)),
        ],
        compiler_params=pltpu.CompilerParams(vmem_limit_bytes=60 * 2**20),
    )(
        pair_first, pair_block[:, 0], pair_second, pair_count,
        jnp.transpose(shifts, (1, 2, 0)), anchors, images, near_table, forward,
    )
    recv = lax.all_to_all(send, "date", split_axis=0, concat_axis=0, tiled=True)
    recv, firsts, seconds = lax.optimization_barrier((recv, firsts, seconds))
    result = pl.pallas_call(
        match_kernel,
        out_shape=jax.ShapeDtypeStruct((blocks, 4, columns), F32),
        in_specs=[vmem] * 8,
        out_specs=vmem,
        scratch_shapes=[
            pltpu.VMEM((dates, length + 2 * SMAX, columns), F32),
            pltpu.VMEM((blocks * 8, columns), F32),
            pltpu.VMEM((8, columns), jnp.int32),
            pltpu.SMEM((8, columns), jnp.int32),
            pltpu.SMEM((CHIP + BATCH,), jnp.int32),
            pltpu.VMEM((BATCH * length, columns), BF16),
            pltpu.VMEM((BATCH * length, columns), BF16),
            pltpu.VMEM((CHIP + 8, columns), F32),
            pltpu.VMEM((CHIP + 8, columns), F32),
            pltpu.VMEM((CHIP + 8, columns), F32),
            pltpu.SemaphoreType.DMA,
        ],
        compiler_params=params,
    )(recv, images, above, below, far_table, forward, form, across)
    result = lax.all_to_all(result, "date", split_axis=0, concat_axis=0, tiled=True)
    offsets, series = pl.pallas_call(
        series_kernel,
        out_shape=(
            jax.ShapeDtypeStruct((2, 2, slots), F32),
            jax.ShapeDtypeStruct((2, 2, dates), F32),
        ),
        in_specs=[vmem] * 4,
        out_specs=(vmem, vmem),
        compiler_params=params,
    )(own, result.reshape(blocks * 4, columns), firsts, seconds)
    return jnp.transpose(offsets, (2, 0, 1)), series


def solution(mesh):
    return jax.shard_map(
        body,
        mesh=mesh,
        in_specs=(
            P("date", "strip", None),
            P(None, "strip", "date", None),
            P("date"),
            P("date", None),
            P("date"),
            P("date"),
            P("date", None, "strip"),
            P("strip"),
        ),
        out_specs=(P("date", None, "strip"), P(None, "strip", "date")),
        check_vma=False,
    )
```

```python
import math

import jax
import jax.numpy as jnp
import ml_dtypes
import numpy as np
from jax import lax
from jax.experimental import pallas as pl
from jax.experimental.pallas import tpu as pltpu
from jax.sharding import PartitionSpec as P

SMAX = 8
CHIP = 64
LANES = 128
BATCH = 32
F32 = jnp.float32
BF16 = jnp.bfloat16


def make_tables():
    half = CHIP // 2
    counter = np.arange(CHIP)
    freq = counter % half
    def basis(places, length):
        turn = 2.0 * math.pi * freq[:, None] * places[None, :] / length
        value = np.where(counter[:, None] < half, np.cos(turn), np.sin(turn))
        value[half] = np.cos(2.0 * math.pi * half * places / length)
        return value
    scale = np.where(freq == 0, 1.0, math.sqrt(2.0))[:, None]
    forward = basis(counter, CHIP) * scale
    cosine, sine = forward[:half].T, forward[half:].T
    zero = np.zeros((CHIP, half))
    def spread(block):
        return np.concatenate([np.concatenate([block, zero], 1), np.concatenate([zero, block], 1)], 0)
    nyquist = cosine.copy(); nyquist[:, 0] = sine[:, 0]
    plain = sine.copy(); plain[:, 0] = 0.0
    near = np.concatenate([spread(cosine), spread(sine)], 1)
    far = np.concatenate([spread(cosine), spread(nyquist), spread(plain), spread(plain)], 1)
    places = np.arange(2 * CHIP)
    displace = ((places + CHIP) % (2 * CHIP) - CHIP) * 0.5
    wave = basis(places, 2 * CHIP)
    form = (wave * displace) @ wave.T / (2 * CHIP)
    cc, cs, sc, ss = form[:half, :half], form[:half, half:], form[half:, :half], form[half:, half:]
    two = np.eye(2)
    across = np.block([[np.kron(two, cc), np.kron(two, cs)], [np.kron(two, sc), np.kron(two, ss)]])
    tables = (near, far, forward, form, across)
    return tuple(a.astype(ml_dtypes.bfloat16) for a in tables)


def dot(a, b):
    return lax.dot_general(a, b, (((1,), (0,)), ((), ())), preferred_element_type=F32)


def dot_nt(a, b):
    return lax.dot_general(a, b, (((1,), (1,)), ((), ())), preferred_element_type=F32)


def parts_of(value, count):
    parts = []
    for _ in range(count):
        part = value.astype(BF16)
        parts.append(part)
        value = value - part.astype(F32)
    return parts


def level_lanes():
    lane = lax.broadcasted_iota(jnp.int32, (1, LANES), 1)
    return jnp.where((lane < CHIP) & (lane % (CHIP // 2) == 0), 1.0 / CHIP, 0.0)


def pack_kernel(
    first_hbm, block_hbm, second_hbm, count_hbm, shifts_hbm, anchors_hbm, images_hbm,
    table_hbm, forward_hbm,
    send_ref, own_ref, images_ref, table_ref, forward_ref,
    first_ref, block_ref, second_ref, count_ref, shifts_ref, anchors_ref,
    near_ref, facts_ref, tally_ref, where_ref, sems,
):
    dates = images_ref.shape[0]
    blocks = send_ref.shape[0]
    slots = first_ref.shape[0]
    copies = [
        pltpu.make_async_copy(source, target, sems.at[index])
        for index, (source, target) in enumerate(
            (
                (anchors_hbm, anchors_ref), (first_hbm, first_ref), (block_hbm, block_ref),
                (second_hbm, second_ref), (count_hbm, count_ref), (shifts_hbm, shifts_ref),
                (table_hbm, table_ref), (forward_hbm, forward_ref), (images_hbm, images_ref),
            )
        )
    ]
    for copy in copies:
        copy.start()
    facts_ref[...] = jnp.zeros(facts_ref.shape, F32)
    for block in range(blocks):
        tally_ref[block] = 0
    for copy in copies[:6]:
        copy.wait()
    place = lax.broadcasted_iota(jnp.int32, (1, LANES), 1)
    row8 = lax.broadcasted_iota(jnp.int32, (8, LANES), 0)
    lane8 = lax.broadcasted_iota(jnp.int32, (8, LANES), 1) % CHIP
    me = lax.axis_index("date")
    for slot in range(slots):
        block = block_ref[slot]
        rank = tally_ref[block]
        tally_ref[block] = rank + 1
        where_ref[slot] = rank
        live = jnp.where(slot < count_ref[0], 1, 0)
        values = [jnp.where(live > 0, second_ref[slot] + 1, 0)]
        for chip in range(2):
            start = shifts_ref[1, chip, slot] + anchors_ref[chip] - chip * CHIP
            values += [shifts_ref[0, chip, slot], start]
        values += [first_ref[slot], shifts_ref[1, 0, slot], shifts_ref[1, 1, slot]]
        fact = jnp.zeros((8, LANES), jnp.int32)
        for index, value in enumerate(values):
            fact = jnp.where(row8 == index, value, fact)
        fact = jnp.where(lane8 == rank * blocks + me, fact, 0)
        facts_ref[rank, pl.ds(pl.multiple_of(block * 8, 8), 8), :] = fact.astype(F32)
        own = jnp.where(place == 0, block, jnp.where(live > 0, rank * blocks, -1))
        own_ref[slot : slot + 1, :] = own.astype(F32)
    row = lax.broadcasted_iota(jnp.int32, (LANES, LANES), 0)
    lane = lax.broadcasted_iota(jnp.int32, (LANES, LANES), 1)
    column = lane + jnp.where(lane < CHIP, anchors_ref[0], anchors_ref[1] - CHIP)
    pick = (row == column).astype(F32).astype(BF16)
    for copy in copies[6:8]:
        copy.wait()
    table = dot(pick, table_ref[...]).astype(BF16)
    level = level_lanes()
    copies[-1].wait()
    section = dot(images_ref[...].reshape(dates * CHIP, LANES), table)
    parts = []
    for date in range(dates):
        part = section[date * CHIP : (date + 1) * CHIP]
        parts.append((part - level * jnp.sum(part, axis=0, keepdims=True)).astype(BF16))
    for date in range(0, dates, 2):
        pair = dot(forward_ref[...], jnp.concatenate(parts[date : date + 2], axis=1)).astype(BF16)
        near_ref[date] = pair[:, :LANES]
        near_ref[date + 1] = pair[:, LANES:]
    for slot in range(slots):
        at = pl.multiple_of(where_ref[slot] * CHIP, CHIP)
        send_ref[block_ref[slot], pl.ds(at, CHIP), :] = near_ref[first_ref[slot]]
    send_ref[:, 2 * CHIP : 2 * CHIP + 8, :] = (
        (facts_ref[0] + facts_ref[1]).reshape(blocks, 8, LANES).astype(BF16)
    )


def match_kernel(
    recv_ref, images_ref, above_ref, below_ref,
    table_ref, forward_ref, form_ref, across_ref, out_ref,
    framed_ref, whole_ref, scalar_ref, list_ref, data_ref, cross_ref,
    energy_ref, tall_ref, wide_ref, copy_sem,
):
    blocks = recv_ref.shape[0]
    dates = images_ref.shape[0]
    half = CHIP // 2
    fact = recv_ref[0, 2 * CHIP : 2 * CHIP + 8, :].astype(F32)
    for block in range(1, blocks):
        fact = fact + recv_ref[block, 2 * CHIP : 2 * CHIP + 8, :].astype(F32)
    whole_ref[...] = fact.astype(jnp.int32)
    copy = pltpu.make_async_copy(whole_ref, scalar_ref, copy_sem)
    copy.start()
    framed_ref[:, :SMAX, :] = above_ref[...].astype(F32)
    framed_ref[:, SMAX : SMAX + CHIP, :] = images_ref[...].astype(F32)
    framed_ref[:, SMAX + CHIP :, :] = below_ref[...].astype(F32)
    for ref in (energy_ref, tall_ref, wide_ref):
        ref[...] = jnp.zeros(ref.shape, F32)
    copy.wait()

    count = 0
    for slot in range(2 * blocks):
        list_ref[count] = slot
        count = count + jnp.minimum(scalar_ref[0, slot], 1)
    spare = CHIP
    for extra in range(BATCH):
        list_ref[count + extra] = spare
    lane = lax.broadcasted_iota(jnp.int32, (1, LANES), 1)
    low = lane < CHIP
    level = level_lanes()
    turn_sign = jnp.where(lane % half == 0, 0.0, jnp.where(low, 1.0, -1.0))
    corner = jnp.where((lane % half == 0) & (lane >= CHIP), 1.0, 0.0)
    top_row = lax.broadcasted_iota(jnp.int32, (8, LANES), 0) == 0

    def one_batch(turn, carry):
        rows_of = []
        near_of = []
        for s in range(BATCH):
            slot = list_ref[turn * BATCH + s]
            rows_of.append(slot)
            source = jnp.where(slot == spare, 0, slot)
            rank = jnp.where(source >= blocks, 1, 0)
            near_of.append((source - rank * blocks, pl.multiple_of(rank * CHIP, CHIP)))
            second = jnp.maximum(scalar_ref[0, source] - 1, 0)
            pieces = []
            starts = []
            for chip in range(2):
                down = scalar_ref[1 + 2 * chip, source] + SMAX
                start = scalar_ref[2 + 2 * chip, source]
                piece = framed_ref[second, pl.ds(down, CHIP), :]
                pieces.append(pltpu.roll(piece, lax.rem(LANES - start, LANES), 1))
                starts.append(start)
            column = lane + jnp.where(low, starts[0], starts[1])
            inside = (column >= 0) & (column < LANES)
            window = jnp.where(low, pieces[0], pieces[1])
            data_ref[s * CHIP : (s + 1) * CHIP, :] = jnp.where(inside, window, 0.0).astype(BF16)
        section = dot(data_ref[...], table_ref[...])
        crosses = []
        for s in range(BATCH):
            part = section[s * CHIP : (s + 1) * CHIP, :LANES]
            part = part - level * jnp.sum(part, axis=0, keepdims=True)
            other = section[s * CHIP : (s + 1) * CHIP, LANES:]
            far = dot(forward_ref[...], jnp.concatenate([part, other], axis=1).astype(BF16))
            block, at = near_of[s]
            near = recv_ref[block, pl.ds(at, CHIP), :].astype(F32)
            turned = pltpu.roll(near, CHIP, 1) * turn_sign
            top, low_rows = near[:half], near[half:]
            top_turned, low_turned = turned[:half], turned[half:]
            p, q = far[:half, :LANES], far[:half, LANES:]
            p_low, q_low = far[half:, :LANES], far[half:, LANES:]
            first = top * p + top_turned * q
            second = low_rows * p_low + low_turned * q_low
            upper = first + second
            lower = (low_rows * p + low_turned * q) - (top * p_low + top_turned * q_low)
            upper = jnp.concatenate([jnp.where(top_row, first[:8], upper[:8]), upper[8:]], axis=0)
            lower = jnp.concatenate([jnp.where(top_row, second[:8], lower[:8]), lower[8:]], axis=0)
            cross = jnp.concatenate([upper, lower], axis=0)
            crosses.append(cross)
            cross_ref[s * CHIP : (s + 1) * CHIP, :] = cross.astype(BF16)
        wide = dot(cross_ref[...], across_ref[...])
        for s in range(0, BATCH, 2):
            pair = [cross_ref[r * CHIP : (r + 1) * CHIP, :] for r in (s, s + 1)]
            tall = dot(form_ref[...], jnp.concatenate(pair, axis=1))
            for r in range(2):
                cross = crosses[s + r]
                power = cross * cross
                tall_r = cross * tall[:, r * LANES : (r + 1) * LANES]
                wide_r = cross * wide[(s + r) * CHIP : (s + r + 1) * CHIP]
                at = pl.ds(rows_of[s + r], 1)
                energy_ref[at, :] = 0.5 * (
                    jnp.sum(power, axis=0, keepdims=True)
                    + power[:1] + corner * power[half : half + 1]
                )
                tall_ref[at, :] = jnp.sum(tall_r, axis=0, keepdims=True)
                wide_ref[at, :] = 0.5 * (jnp.sum(wide_r, axis=0, keepdims=True) + wide_r[:1])
        return carry

    lax.fori_loop(0, (count + BATCH - 1) // BATCH, one_batch, 0)

    lane8 = lax.broadcasted_iota(jnp.int32, (8, LANES), 1)
    row8 = lax.broadcasted_iota(jnp.int32, (8, LANES), 0)
    weights = jnp.where((row8 == 1) | ((lane8 % half == 0) & (lane8 < CHIP)), 1.0, 0.5)
    even = lane // half % 2 == 0
    stack = []
    for ref in (energy_ref, tall_ref, wide_ref):
        value = ref[:CHIP, :]
        stack += [jnp.where(even, value, 0.0), jnp.where(even, 0.0, value)]
    weights = weights.astype(BF16)
    found = sum(dot_nt(weights, part) for part in parts_of(jnp.concatenate(stack, axis=0), 3))
    norm = found[0:1, :LANES] + 1e-6
    tall = found[0:1, LANES : 2 * LANES] / norm
    wide = found[1:2, 2 * LANES :] / norm
    live = fact[0:1] > 0.5
    down = jnp.where(live, jnp.where(low, fact[1:2], fact[3:4]) + tall, 0.0)
    across = jnp.where(live, jnp.where(low, fact[6:7], fact[7:8]) + wide, 0.0)
    row = lax.broadcasted_iota(jnp.int32, (LANES, LANES), 0)
    row = jnp.where(row < CHIP, -1, row % dates).astype(F32)
    chosen = (row == fact[0:1] - 1.0).astype(F32).astype(BF16)
    value = jnp.where(row8 < 2, down, across)
    value = jnp.where((row8 < 4) & ((row8 % 2 == 0) == (lane8 < CHIP)), value, 0.0)
    sums = dot_nt(jnp.concatenate(parts_of(value, 3), axis=0), chosen)
    sums = sums[:8] + sums[8:16] + sums[16:24]
    sums = jnp.where((lane8 - CHIP) // dates == row8, sums, 0.0)
    sums = jnp.sum(sums, axis=0, keepdims=True)
    sums = jnp.where(low, fact[5:6], sums)
    result = jnp.where(row8 == 0, down, jnp.where(row8 == 1, across, sums))
    for block in range(blocks):
        out_ref[block] = result[:4]


def series_kernel(
    own_ref, result_ref, firsts_ref, seconds_ref, offsets_ref, series_ref
):
    blocks = result_ref.shape[0] // 4
    slots = own_ref.shape[0]
    dates = seconds_ref.shape[0]
    me = lax.axis_index("date").astype(F32)
    own = own_ref[...]
    partner = lax.broadcasted_iota(jnp.int32, (slots, blocks), 1).astype(F32)
    partner = (own[:, 0:1] == partner).astype(F32).astype(BF16)
    lane = lax.broadcasted_iota(jnp.int32, (slots, LANES), 1)
    mine = lane.astype(F32) - me == own[:, 1:2] + jnp.where(lane < CHIP, 0.0, float(CHIP))
    mine = mine & (own[:, 1:2] >= 0.0)
    facts = result_ref[pl.ds(2, blocks, stride=4), :]
    low = lax.broadcasted_iota(jnp.int32, (blocks, LANES), 1) < CHIP
    first = jnp.where(low, facts, pltpu.roll(facts, CHIP, 1))
    lane8 = lax.broadcasted_iota(jnp.int32, (8, LANES), 1)
    row8 = lax.broadcasted_iota(jnp.int32, (8, LANES), 0)
    chips = (lane8 // CHIP == row8).astype(F32).astype(BF16)
    pieces = ((lane8 - CHIP) // dates == row8).astype(F32).astype(BF16)
    total = jnp.concatenate(
        [jnp.sum(seconds_ref[date] * facts, axis=0, keepdims=True) for date in range(dates)],
        axis=0,
    )
    gained = sum(dot_nt(pieces, part) for part in parts_of(total, 3))
    for axis in range(2):
        rows = result_ref[pl.ds(axis, blocks, stride=4), :]
        value = sum(dot(partner, part) for part in parts_of(rows, 3))
        value = jnp.where(mine, value, 0.0)
        value = sum(dot_nt(chips, part) for part in parts_of(value, 3))
        offsets_ref[axis] = value[:2]
        total = jnp.zeros((dates, LANES), F32)
        for date in range(dates):
            here = jnp.sum(jnp.where(first == date, rows, 0.0), axis=0, keepdims=True)
            total = total + firsts_ref[axis, date] * here
        lost = sum(dot_nt(chips, part) for part in parts_of(total, 3))
        series_ref[axis] = gained[2 * axis : 2 * axis + 2] - lost[:2]


def body(images, inverse_blocks, pair_first, pair_block, pair_second, pair_count, shifts, anchors):
    blocks = lax.axis_size("date")
    strips = lax.axis_size("strip")
    dates, length, columns = images.shape
    slots = pair_first.shape[0]
    hbm = pl.BlockSpec(memory_space=pltpu.HBM)
    vmem = pl.BlockSpec(memory_space=pltpu.VMEM)
    params = pltpu.CompilerParams(vmem_limit_bytes=48 * 2**20)
    ends = strips - 1
    above = lax.ppermute(
        images[:, length - SMAX :, :], "strip", [(i, i + 1) for i in range(ends)]
    )
    below = lax.ppermute(images[:, :SMAX, :], "strip", [(i + 1, i) for i in range(ends)])
    turned = inverse_blocks.reshape(2, 2, dates, blocks, dates).transpose(0, 4, 2, 1, 3)
    turned = jnp.concatenate([turned, turned], axis=4)
    turned = jnp.pad(turned, ((0, 0),) * 4 + ((0, CHIP - 2 * blocks),))
    firsts = turned.reshape(2, dates, dates, LANES)
    seconds = inverse_blocks.reshape(2, 2, dates, blocks, dates).transpose(2, 3, 0, 1, 4)
    seconds = jnp.pad(seconds.reshape(dates, blocks, 4 * dates), ((0, 0), (0, 0), (CHIP, 0)))
    near_table, far_table, forward, form, across = [jnp.asarray(t) for t in make_tables()]
    send, own = pl.pallas_call(
        pack_kernel,
        out_shape=(
            jax.ShapeDtypeStruct((blocks, 2 * length + 8, columns), BF16),
            jax.ShapeDtypeStruct((slots, columns), F32),
        ),
        in_specs=[hbm] * 9,
        out_specs=(vmem, vmem),
        scratch_shapes=[
            pltpu.VMEM(images.shape, BF16),
            pltpu.VMEM(near_table.shape, BF16),
            pltpu.VMEM(forward.shape, BF16),
            pltpu.SMEM((slots,), jnp.int32),
            pltpu.SMEM((slots,), jnp.int32),
            pltpu.SMEM((slots,), jnp.int32),
            pltpu.SMEM((1,), jnp.int32),
            pltpu.SMEM((2, 2, slots), jnp.int32),
            pltpu.SMEM((2,), jnp.int32),
            pltpu.VMEM((dates, length, columns), BF16),
            pltpu.VMEM((2, blocks * 8, columns), F32),
            pltpu.SMEM((blocks,), jnp.int32),
            pltpu.SMEM((slots,), jnp.int32),
            pltpu.SemaphoreType.DMA((9,)),
        ],
        compiler_params=pltpu.CompilerParams(vmem_limit_bytes=60 * 2**20),
    )(
        pair_first, pair_block[:, 0], pair_second, pair_count,
        jnp.transpose(shifts, (1, 2, 0)), anchors, images, near_table, forward,
    )
    recv = lax.all_to_all(send, "date", split_axis=0, concat_axis=0, tiled=True)
    recv, firsts, seconds = lax.optimization_barrier((recv, firsts, seconds))
    result = pl.pallas_call(
        match_kernel,
        out_shape=jax.ShapeDtypeStruct((blocks, 4, columns), F32),
        in_specs=[vmem] * 8,
        out_specs=vmem,
        scratch_shapes=[
            pltpu.VMEM((dates, length + 2 * SMAX, columns), F32),
            pltpu.VMEM((8, columns), jnp.int32),
            pltpu.SMEM((8, columns), jnp.int32),
            pltpu.SMEM((CHIP + BATCH,), jnp.int32),
            pltpu.VMEM((BATCH * length, columns), BF16),
            pltpu.VMEM((BATCH * length, columns), BF16),
            pltpu.VMEM((CHIP + 8, columns), F32),
            pltpu.VMEM((CHIP + 8, columns), F32),
            pltpu.VMEM((CHIP + 8, columns), F32),
            pltpu.SemaphoreType.DMA,
        ],
        compiler_params=params,
    )(recv, images, above, below, far_table, forward, form, across)
    result = lax.all_to_all(result, "date", split_axis=0, concat_axis=0, tiled=True)
    offsets, series = pl.pallas_call(
        series_kernel,
        out_shape=(
            jax.ShapeDtypeStruct((2, 2, slots), F32),
            jax.ShapeDtypeStruct((2, 2, dates), F32),
        ),
        in_specs=[vmem] * 4,
        out_specs=(vmem, vmem),
        compiler_params=params,
    )(own, result.reshape(blocks * 4, columns), firsts, seconds)
    return jnp.transpose(offsets, (2, 0, 1)), series


def solution(mesh):
    return jax.shard_map(
        body,
        mesh=mesh,
        in_specs=(
            P("date", "strip", None),
            P(None, "strip", "date", None),
            P("date"),
            P("date", None),
            P("date"),
            P("date"),
            P("date", None, "strip"),
            P("strip"),
        ),
        out_specs=(P("date", None, "strip"), P(None, "strip", "date")),
        check_vma=False,
    )
```

```python
import math

import jax
import jax.numpy as jnp
import ml_dtypes
import numpy as np
from jax import lax
from jax.experimental import pallas as pl
from jax.experimental.pallas import tpu as pltpu
from jax.sharding import PartitionSpec as P

SMAX = 8
CHIP = 64
LANES = 128
BATCH = 32
F32 = jnp.float32
BF16 = jnp.bfloat16


def make_tables():
    half = CHIP // 2
    counter = np.arange(CHIP)
    freq = counter % half
    def basis(places, length):
        turn = 2.0 * math.pi * freq[:, None] * places[None, :] / length
        value = np.where(counter[:, None] < half, np.cos(turn), np.sin(turn))
        value[half] = np.cos(2.0 * math.pi * half * places / length)
        return value
    scale = np.where(freq == 0, 1.0, math.sqrt(2.0))[:, None]
    forward = basis(counter, CHIP) * scale
    cosine, sine = forward[:half].T, forward[half:].T
    zero = np.zeros((CHIP, half))
    def spread(block):
        return np.concatenate([np.concatenate([block, zero], 1), np.concatenate([zero, block], 1)], 0)
    nyquist = cosine.copy(); nyquist[:, 0] = sine[:, 0]
    plain = sine.copy(); plain[:, 0] = 0.0
    near = np.concatenate([spread(cosine), spread(sine)], 1)
    far = np.concatenate([spread(cosine), spread(nyquist), spread(plain), spread(plain)], 1)
    places = np.arange(2 * CHIP)
    displace = ((places + CHIP) % (2 * CHIP) - CHIP) * 0.5
    wave = basis(places, 2 * CHIP)
    form = (wave * displace) @ wave.T / (2 * CHIP)
    cc, cs, sc, ss = form[:half, :half], form[:half, half:], form[half:, :half], form[half:, half:]
    two = np.eye(2)
    across = np.block([[np.kron(two, cc), np.kron(two, cs)], [np.kron(two, sc), np.kron(two, ss)]])
    tables = (near, far, forward, form, across)
    return tuple(a.astype(ml_dtypes.bfloat16) for a in tables)


def dot(a, b):
    return lax.dot_general(a, b, (((1,), (0,)), ((), ())), preferred_element_type=F32)


def dot_nt(a, b):
    return lax.dot_general(a, b, (((1,), (1,)), ((), ())), preferred_element_type=F32)


def parts_of(value, count):
    parts = []
    for _ in range(count):
        part = value.astype(BF16)
        parts.append(part)
        value = value - part.astype(F32)
    return parts


def level_lanes():
    lane = lax.broadcasted_iota(jnp.int32, (1, LANES), 1)
    return jnp.where((lane < CHIP) & (lane % (CHIP // 2) == 0), 1.0 / CHIP, 0.0)


def pack_kernel(
    first_hbm, block_hbm, second_hbm, count_hbm, shifts_hbm, anchors_hbm, images_hbm,
    table_hbm, forward_hbm,
    send_ref, own_ref, images_ref, table_ref, forward_ref,
    first_ref, block_ref, second_ref, count_ref, shifts_ref, anchors_ref,
    near_ref, facts_ref, tally_ref, where_ref, sems,
):
    dates = images_ref.shape[0]
    blocks = send_ref.shape[0]
    slots = first_ref.shape[0]
    copies = [
        pltpu.make_async_copy(source, target, sems.at[index])
        for index, (source, target) in enumerate(
            (
                (anchors_hbm, anchors_ref), (first_hbm, first_ref), (block_hbm, block_ref),
                (second_hbm, second_ref), (count_hbm, count_ref), (shifts_hbm, shifts_ref),
                (table_hbm, table_ref), (forward_hbm, forward_ref), (images_hbm, images_ref),
            )
        )
    ]
    for copy in copies:
        copy.start()
    facts_ref[...] = jnp.zeros(facts_ref.shape, F32)
    for block in range(blocks):
        tally_ref[block] = 0
    for copy in copies[:6]:
        copy.wait()
    place = lax.broadcasted_iota(jnp.int32, (1, LANES), 1)
    for slot in range(slots):
        block = block_ref[slot]
        rank = tally_ref[block]
        tally_ref[block] = rank + 1
        where_ref[slot] = rank
        live = jnp.where(slot < count_ref[0], 1, 0)
        values = [live, second_ref[slot]]
        for chip in range(2):
            start = shifts_ref[1, chip, slot] + anchors_ref[chip] - chip * CHIP
            values += [shifts_ref[0, chip, slot], start]
        values += [first_ref[slot], shifts_ref[1, 0, slot], shifts_ref[1, 1, slot]]
        fact = jnp.zeros((1, LANES), jnp.int32)
        for index, value in enumerate(values):
            fact = jnp.where(place == index, value, fact)
        facts_ref[pl.ds(block * 8 + rank, 1), :] = fact.astype(F32)
        own = jnp.where(place == 0, block, jnp.where(live > 0, rank * blocks, -1))
        own_ref[slot : slot + 1, :] = own.astype(F32)
    row = lax.broadcasted_iota(jnp.int32, (LANES, LANES), 0)
    lane = lax.broadcasted_iota(jnp.int32, (LANES, LANES), 1)
    column = lane + jnp.where(lane < CHIP, anchors_ref[0], anchors_ref[1] - CHIP)
    pick = (row == column).astype(F32).astype(BF16)
    for copy in copies[6:8]:
        copy.wait()
    table = dot(pick, table_ref[...]).astype(BF16)
    level = level_lanes()
    copies[-1].wait()
    section = dot(images_ref[...].reshape(dates * CHIP, LANES), table)
    parts = []
    for date in range(dates):
        part = section[date * CHIP : (date + 1) * CHIP]
        parts.append((part - level * jnp.sum(part, axis=0, keepdims=True)).astype(BF16))
    for date in range(0, dates, 2):
        pair = dot(forward_ref[...], jnp.concatenate(parts[date : date + 2], axis=1)).astype(BF16)
        near_ref[date] = pair[:, :LANES]
        near_ref[date + 1] = pair[:, LANES:]
    for slot in range(slots):
        at = pl.multiple_of(where_ref[slot] * CHIP, CHIP)
        send_ref[block_ref[slot], pl.ds(at, CHIP), :] = near_ref[first_ref[slot]]
    send_ref[:, 2 * CHIP : 2 * CHIP + 8, :] = (
        facts_ref[...].reshape(blocks, 8, LANES).astype(BF16)
    )


def match_kernel(
    recv_ref, images_ref, above_ref, below_ref,
    table_ref, forward_ref, form_ref, across_ref, out_ref,
    framed_ref, facts_ref, whole_ref, scalar_ref, list_ref, data_ref, cross_ref,
    energy_ref, tall_ref, wide_ref, copy_sem,
):
    blocks = recv_ref.shape[0]
    dates = images_ref.shape[0]
    half = CHIP // 2
    facts_ref[...] = recv_ref[:, 2 * CHIP : 2 * CHIP + 8, :].astype(F32).reshape(blocks * 8, LANES)
    whole = [facts_ref[pl.ds(rank, blocks, stride=8), :].astype(BF16) for rank in range(2)]
    if blocks < CHIP // 2:
        whole.append(jnp.zeros((CHIP - 2 * blocks, LANES), BF16))
    lane16 = lax.broadcasted_iota(jnp.int32, (16, LANES), 1)
    row16 = lax.broadcasted_iota(jnp.int32, (16, LANES), 0)
    choose = (lane16 == row16).astype(F32).astype(BF16)
    fact = dot_nt(choose, jnp.concatenate(whole + whole, axis=0))
    whole_ref[...] = fact[:8].astype(jnp.int32)
    copy = pltpu.make_async_copy(whole_ref, scalar_ref, copy_sem)
    copy.start()
    framed_ref[:, :SMAX, :] = above_ref[...].astype(F32)
    framed_ref[:, SMAX : SMAX + CHIP, :] = images_ref[...].astype(F32)
    framed_ref[:, SMAX + CHIP :, :] = below_ref[...].astype(F32)
    for ref in (energy_ref, tall_ref, wide_ref):
        ref[...] = jnp.zeros(ref.shape, F32)
    copy.wait()

    count = 0
    for slot in range(2 * blocks):
        list_ref[count] = slot
        count = count + scalar_ref[0, slot]
    spare = CHIP
    for extra in range(BATCH):
        list_ref[count + extra] = spare
    lane = lax.broadcasted_iota(jnp.int32, (1, LANES), 1)
    low = lane < CHIP
    level = level_lanes()
    turn_sign = jnp.where(lane % half == 0, 0.0, jnp.where(low, 1.0, -1.0))
    corner = jnp.where((lane % half == 0) & (lane >= CHIP), 1.0, 0.0)
    top_row = lax.broadcasted_iota(jnp.int32, (8, LANES), 0) == 0

    def one_batch(turn, carry):
        rows_of = []
        near_of = []
        for s in range(BATCH):
            slot = list_ref[turn * BATCH + s]
            rows_of.append(slot)
            source = jnp.where(slot == spare, 0, slot)
            rank = jnp.where(source >= blocks, 1, 0)
            near_of.append((source - rank * blocks, pl.multiple_of(rank * CHIP, CHIP)))
            second = scalar_ref[1, source]
            pieces = []
            starts = []
            for chip in range(2):
                down = scalar_ref[2 + 2 * chip, source] + SMAX
                start = scalar_ref[3 + 2 * chip, source]
                piece = framed_ref[second, pl.ds(down, CHIP), :]
                pieces.append(pltpu.roll(piece, lax.rem(LANES - start, LANES), 1))
                starts.append(start)
            column = lane + jnp.where(low, starts[0], starts[1])
            inside = (column >= 0) & (column < LANES)
            window = jnp.where(low, pieces[0], pieces[1])
            data_ref[s * CHIP : (s + 1) * CHIP, :] = jnp.where(inside, window, 0.0).astype(BF16)
        section = dot(data_ref[...], table_ref[...])
        crosses = []
        for s in range(BATCH):
            part = section[s * CHIP : (s + 1) * CHIP, :LANES]
            part = part - level * jnp.sum(part, axis=0, keepdims=True)
            other = section[s * CHIP : (s + 1) * CHIP, LANES:]
            far = dot(forward_ref[...], jnp.concatenate([part, other], axis=1).astype(BF16))
            block, at = near_of[s]
            near = recv_ref[block, pl.ds(at, CHIP), :].astype(F32)
            turned = pltpu.roll(near, CHIP, 1) * turn_sign
            top, low_rows = near[:half], near[half:]
            top_turned, low_turned = turned[:half], turned[half:]
            p, q = far[:half, :LANES], far[:half, LANES:]
            p_low, q_low = far[half:, :LANES], far[half:, LANES:]
            first = top * p + top_turned * q
            second = low_rows * p_low + low_turned * q_low
            upper = first + second
            lower = (low_rows * p + low_turned * q) - (top * p_low + top_turned * q_low)
            upper = jnp.concatenate([jnp.where(top_row, first[:8], upper[:8]), upper[8:]], axis=0)
            lower = jnp.concatenate([jnp.where(top_row, second[:8], lower[:8]), lower[8:]], axis=0)
            cross = jnp.concatenate([upper, lower], axis=0)
            crosses.append(cross)
            cross_ref[s * CHIP : (s + 1) * CHIP, :] = cross.astype(BF16)
        wide = dot(cross_ref[...], across_ref[...])
        for s in range(0, BATCH, 2):
            pair = [cross_ref[r * CHIP : (r + 1) * CHIP, :] for r in (s, s + 1)]
            tall = dot(form_ref[...], jnp.concatenate(pair, axis=1))
            for r in range(2):
                cross = crosses[s + r]
                power = cross * cross
                tall_r = cross * tall[:, r * LANES : (r + 1) * LANES]
                wide_r = cross * wide[(s + r) * CHIP : (s + r + 1) * CHIP]
                at = pl.ds(rows_of[s + r], 1)
                energy_ref[at, :] = 0.5 * (
                    jnp.sum(power, axis=0, keepdims=True)
                    + power[:1] + corner * power[half : half + 1]
                )
                tall_ref[at, :] = jnp.sum(tall_r, axis=0, keepdims=True)
                wide_ref[at, :] = 0.5 * (jnp.sum(wide_r, axis=0, keepdims=True) + wide_r[:1])
        return carry

    lax.fori_loop(0, (count + BATCH - 1) // BATCH, one_batch, 0)

    lane8 = lax.broadcasted_iota(jnp.int32, (8, LANES), 1)
    row8 = lax.broadcasted_iota(jnp.int32, (8, LANES), 0)
    weights = jnp.where((row8 == 1) | ((lane8 % half == 0) & (lane8 < CHIP)), 1.0, 0.5)
    even = lane // half % 2 == 0
    stack = []
    for ref in (energy_ref, tall_ref, wide_ref):
        value = ref[:CHIP, :]
        stack += [jnp.where(even, value, 0.0), jnp.where(even, 0.0, value)]
    weights = weights.astype(BF16)
    found = sum(dot_nt(weights, part) for part in parts_of(jnp.concatenate(stack, axis=0), 2))
    norm = found[0:1, :LANES] + 1e-6
    tall = found[0:1, LANES : 2 * LANES] / norm
    wide = found[1:2, 2 * LANES :] / norm
    live = fact[0:1] > 0.5
    down = jnp.where(live, jnp.where(low, fact[2:3], fact[4:5]) + tall, 0.0)
    across = jnp.where(live, jnp.where(low, fact[7:8], fact[8:9]) + wide, 0.0)
    row = lax.broadcasted_iota(jnp.int32, (LANES, LANES), 0)
    row = jnp.where(row < CHIP, -1, row % dates).astype(F32)
    chosen = (row == fact[1:2]).astype(F32).astype(BF16)
    value = jnp.where(row8 < 2, down, across)
    value = jnp.where((row8 < 4) & ((row8 % 2 == 0) == (lane8 < CHIP)), value, 0.0)
    sums = dot_nt(jnp.concatenate(parts_of(value, 2), axis=0), chosen)
    sums = sums[:8] + sums[8:16]
    sums = jnp.where((lane8 - CHIP) // dates == row8, sums, 0.0)
    sums = jnp.sum(sums, axis=0, keepdims=True)
    sums = jnp.where(low, fact[6:7], sums)
    result = jnp.where(row8 == 0, down, jnp.where(row8 == 1, across, sums))
    for block in range(blocks):
        out_ref[block] = result[:4]


def series_kernel(
    own_ref, result_ref, firsts_ref, seconds_ref, offsets_ref, series_ref
):
    blocks = result_ref.shape[0] // 4
    slots = own_ref.shape[0]
    dates = seconds_ref.shape[0]
    me = lax.axis_index("date").astype(F32)
    own = own_ref[...]
    partner = lax.broadcasted_iota(jnp.int32, (slots, blocks), 1).astype(F32)
    partner = (own[:, 0:1] == partner).astype(F32).astype(BF16)
    lane = lax.broadcasted_iota(jnp.int32, (slots, LANES), 1)
    mine = lane.astype(F32) - me == own[:, 1:2] + jnp.where(lane < CHIP, 0.0, float(CHIP))
    mine = mine & (own[:, 1:2] >= 0.0)
    facts = result_ref[pl.ds(2, blocks, stride=4), :]
    low = lax.broadcasted_iota(jnp.int32, (blocks, LANES), 1) < CHIP
    first = jnp.where(low, facts, pltpu.roll(facts, CHIP, 1))
    lane8 = lax.broadcasted_iota(jnp.int32, (8, LANES), 1)
    row8 = lax.broadcasted_iota(jnp.int32, (8, LANES), 0)
    chips = (lane8 // CHIP == row8).astype(F32).astype(BF16)
    pieces = ((lane8 - CHIP) // dates == row8).astype(F32).astype(BF16)
    total = jnp.concatenate(
        [jnp.sum(seconds_ref[date] * facts, axis=0, keepdims=True) for date in range(dates)],
        axis=0,
    )
    gained = sum(dot_nt(pieces, part) for part in parts_of(total, 2))
    for axis in range(2):
        rows = result_ref[pl.ds(axis, blocks, stride=4), :]
        value = sum(dot(partner, part) for part in parts_of(rows, 2))
        value = jnp.where(mine, value, 0.0)
        value = sum(dot_nt(chips, part) for part in parts_of(value, 2))
        offsets_ref[axis] = value[:2]
        total = jnp.zeros((dates, LANES), F32)
        for date in range(dates):
            here = jnp.sum(jnp.where(first == date, rows, 0.0), axis=0, keepdims=True)
            total = total + firsts_ref[axis, date] * here
        lost = sum(dot_nt(chips, part) for part in parts_of(total, 2))
        series_ref[axis] = gained[2 * axis : 2 * axis + 2] - lost[:2]


def body(images, inverse_blocks, pair_first, pair_block, pair_second, pair_count, shifts, anchors):
    blocks = lax.axis_size("date")
    strips = lax.axis_size("strip")
    dates, length, columns = images.shape
    slots = pair_first.shape[0]
    hbm = pl.BlockSpec(memory_space=pltpu.HBM)
    vmem = pl.BlockSpec(memory_space=pltpu.VMEM)
    params = pltpu.CompilerParams(vmem_limit_bytes=48 * 2**20)
    ends = strips - 1
    above = lax.ppermute(
        images[:, length - SMAX :, :], "strip", [(i, i + 1) for i in range(ends)]
    )
    below = lax.ppermute(images[:, :SMAX, :], "strip", [(i + 1, i) for i in range(ends)])
    turned = inverse_blocks.reshape(2, 2, dates, blocks, dates).transpose(0, 4, 2, 1, 3)
    turned = jnp.concatenate([turned, turned], axis=4)
    turned = jnp.pad(turned, ((0, 0),) * 4 + ((0, CHIP - 2 * blocks),))
    firsts = turned.reshape(2, dates, dates, LANES)
    seconds = inverse_blocks.reshape(2, 2, dates, blocks, dates).transpose(2, 3, 0, 1, 4)
    seconds = jnp.pad(seconds.reshape(dates, blocks, 4 * dates), ((0, 0), (0, 0), (CHIP, 0)))
    near_table, far_table, forward, form, across = [jnp.asarray(t) for t in make_tables()]
    send, own = pl.pallas_call(
        pack_kernel,
        out_shape=(
            jax.ShapeDtypeStruct((blocks, 2 * length + 8, columns), BF16),
            jax.ShapeDtypeStruct((slots, columns), F32),
        ),
        in_specs=[hbm] * 9,
        out_specs=(vmem, vmem),
        scratch_shapes=[
            pltpu.VMEM(images.shape, BF16),
            pltpu.VMEM(near_table.shape, BF16),
            pltpu.VMEM(forward.shape, BF16),
            pltpu.SMEM((slots,), jnp.int32),
            pltpu.SMEM((slots,), jnp.int32),
            pltpu.SMEM((slots,), jnp.int32),
            pltpu.SMEM((1,), jnp.int32),
            pltpu.SMEM((2, 2, slots), jnp.int32),
            pltpu.SMEM((2,), jnp.int32),
            pltpu.VMEM((dates, length, columns), BF16),
            pltpu.VMEM((blocks * 8, columns), F32),
            pltpu.SMEM((blocks,), jnp.int32),
            pltpu.SMEM((slots,), jnp.int32),
            pltpu.SemaphoreType.DMA((9,)),
        ],
        compiler_params=pltpu.CompilerParams(vmem_limit_bytes=60 * 2**20),
    )(
        pair_first, pair_block[:, 0], pair_second, pair_count,
        jnp.transpose(shifts, (1, 2, 0)), anchors, images, near_table, forward,
    )
    recv = lax.all_to_all(send, "date", split_axis=0, concat_axis=0, tiled=True)
    recv, firsts, seconds = lax.optimization_barrier((recv, firsts, seconds))
    result = pl.pallas_call(
        match_kernel,
        out_shape=jax.ShapeDtypeStruct((blocks, 4, columns), F32),
        in_specs=[vmem] * 8,
        out_specs=vmem,
        scratch_shapes=[
            pltpu.VMEM((dates, length + 2 * SMAX, columns), F32),
            pltpu.VMEM((blocks * 8, columns), F32),
            pltpu.VMEM((8, columns), jnp.int32),
            pltpu.SMEM((8, columns), jnp.int32),
            pltpu.SMEM((CHIP + BATCH,), jnp.int32),
            pltpu.VMEM((BATCH * length, columns), BF16),
            pltpu.VMEM((BATCH * length, columns), BF16),
            pltpu.VMEM((CHIP + 8, columns), F32),
            pltpu.VMEM((CHIP + 8, columns), F32),
            pltpu.VMEM((CHIP + 8, columns), F32),
            pltpu.SemaphoreType.DMA,
        ],
        compiler_params=params,
    )(recv, images, above, below, far_table, forward, form, across)
    result = lax.all_to_all(result, "date", split_axis=0, concat_axis=0, tiled=True)
    offsets, series = pl.pallas_call(
        series_kernel,
        out_shape=(
            jax.ShapeDtypeStruct((2, 2, slots), F32),
            jax.ShapeDtypeStruct((2, 2, dates), F32),
        ),
        in_specs=[vmem] * 4,
        out_specs=(vmem, vmem),
        compiler_params=params,
    )(own, result.reshape(blocks * 4, columns), firsts, seconds)
    return jnp.transpose(offsets, (2, 0, 1)), series


def solution(mesh):
    return jax.shard_map(
        body,
        mesh=mesh,
        in_specs=(
            P("date", "strip", None),
            P(None, "strip", "date", None),
            P("date"),
            P("date", None),
            P("date"),
            P("date"),
            P("date", None, "strip"),
            P("strip"),
        ),
        out_specs=(P("date", None, "strip"), P(None, "strip", "date")),
        check_vma=False,
    )
```

```python
import math

import jax
import jax.numpy as jnp
import ml_dtypes
import numpy as np
from jax import lax
from jax.experimental import pallas as pl
from jax.experimental.pallas import tpu as pltpu
from jax.sharding import PartitionSpec as P

SMAX = 8
CHIP = 64
LANES = 128
BATCH = 28
F32 = jnp.float32
BF16 = jnp.bfloat16


def make_tables():
    half = CHIP // 2
    counter = np.arange(CHIP)
    freq = counter % half
    def basis(places, length):
        turn = 2.0 * math.pi * freq[:, None] * places[None, :] / length
        value = np.where(counter[:, None] < half, np.cos(turn), np.sin(turn))
        value[half] = np.cos(2.0 * math.pi * half * places / length)
        return value
    scale = np.where(freq == 0, 1.0, math.sqrt(2.0))[:, None]
    forward = basis(counter, CHIP) * scale
    cosine, sine = forward[:half].T, forward[half:].T
    zero = np.zeros((CHIP, half))
    def spread(block):
        return np.concatenate([np.concatenate([block, zero], 1), np.concatenate([zero, block], 1)], 0)
    nyquist = cosine.copy(); nyquist[:, 0] = sine[:, 0]
    plain = sine.copy(); plain[:, 0] = 0.0
    near = np.concatenate([spread(cosine), spread(sine)], 1)
    far = np.concatenate([spread(cosine), spread(nyquist), spread(plain), spread(plain)], 1)
    places = np.arange(2 * CHIP)
    displace = ((places + CHIP) % (2 * CHIP) - CHIP) * 0.5
    wave = basis(places, 2 * CHIP)
    form = (wave * displace) @ wave.T / (2 * CHIP)
    cc, cs, sc, ss = form[:half, :half], form[:half, half:], form[half:, :half], form[half:, half:]
    two = np.eye(2)
    across = np.block([[np.kron(two, cc), np.kron(two, cs)], [np.kron(two, sc), np.kron(two, ss)]])
    tables = (near, far, forward, form, across)
    return tuple(a.astype(ml_dtypes.bfloat16) for a in tables)


def dot(a, b):
    return lax.dot_general(a, b, (((1,), (0,)), ((), ())), preferred_element_type=F32)


def dot_nt(a, b):
    return lax.dot_general(a, b, (((1,), (1,)), ((), ())), preferred_element_type=F32)


def parts_of(value, count):
    parts = []
    for _ in range(count):
        part = value.astype(BF16)
        parts.append(part)
        value = value - part.astype(F32)
    return parts


def level_lanes():
    lane = lax.broadcasted_iota(jnp.int32, (1, LANES), 1)
    return jnp.where((lane < CHIP) & (lane % (CHIP // 2) == 0), 1.0 / CHIP, 0.0)


def pack_kernel(
    first_hbm, block_hbm, second_hbm, count_hbm, shifts_hbm, anchors_hbm, images_hbm,
    table_hbm, forward_hbm,
    send_ref, own_ref, images_ref, table_ref, forward_ref,
    first_ref, block_ref, second_ref, count_ref, shifts_ref, anchors_ref,
    near_ref, facts_ref, tally_ref, where_ref, sems,
):
    dates = images_ref.shape[0]
    blocks = send_ref.shape[0]
    slots = first_ref.shape[0]
    copies = [
        pltpu.make_async_copy(source, target, sems.at[index])
        for index, (source, target) in enumerate(
            (
                (anchors_hbm, anchors_ref), (first_hbm, first_ref), (block_hbm, block_ref),
                (second_hbm, second_ref), (count_hbm, count_ref), (shifts_hbm, shifts_ref),
                (table_hbm, table_ref), (forward_hbm, forward_ref), (images_hbm, images_ref),
            )
        )
    ]
    for copy in copies:
        copy.start()
    facts_ref[...] = jnp.zeros(facts_ref.shape, F32)
    for block in range(blocks):
        tally_ref[block] = 0
    for copy in copies[:6]:
        copy.wait()
    place = lax.broadcasted_iota(jnp.int32, (1, LANES), 1)
    for slot in range(slots):
        block = block_ref[slot]
        rank = tally_ref[block]
        tally_ref[block] = rank + 1
        where_ref[slot] = rank
        live = jnp.where(slot < count_ref[0], 1, 0)
        values = [live, second_ref[slot]]
        for chip in range(2):
            start = shifts_ref[1, chip, slot] + anchors_ref[chip] - chip * CHIP
            values += [shifts_ref[0, chip, slot], start]
        values += [first_ref[slot], shifts_ref[1, 0, slot], shifts_ref[1, 1, slot]]
        fact = jnp.zeros((1, LANES), jnp.int32)
        for index, value in enumerate(values):
            fact = jnp.where(place == index, value, fact)
        facts_ref[pl.ds(block * 8 + rank, 1), :] = fact.astype(F32)
        own = jnp.where(place == 0, block, jnp.where(live > 0, rank * blocks, -1))
        own_ref[slot : slot + 1, :] = own.astype(F32)
    row = lax.broadcasted_iota(jnp.int32, (LANES, LANES), 0)
    lane = lax.broadcasted_iota(jnp.int32, (LANES, LANES), 1)
    column = lane + jnp.where(lane < CHIP, anchors_ref[0], anchors_ref[1] - CHIP)
    pick = (row == column).astype(F32).astype(BF16)
    for copy in copies[6:8]:
        copy.wait()
    table = dot(pick, table_ref[...]).astype(BF16)
    level = level_lanes()
    copies[-1].wait()
    section = dot(images_ref[...].reshape(dates * CHIP, LANES), table)
    parts = []
    for date in range(dates):
        part = section[date * CHIP : (date + 1) * CHIP]
        parts.append((part - level * jnp.sum(part, axis=0, keepdims=True)).astype(BF16))
    for date in range(0, dates, 2):
        pair = dot(forward_ref[...], jnp.concatenate(parts[date : date + 2], axis=1)).astype(BF16)
        near_ref[date] = pair[:, :LANES]
        near_ref[date + 1] = pair[:, LANES:]
    for slot in range(slots):
        at = pl.multiple_of(where_ref[slot] * CHIP, CHIP)
        send_ref[block_ref[slot], pl.ds(at, CHIP), :] = near_ref[first_ref[slot]]
    send_ref[:, 2 * CHIP : 2 * CHIP + 8, :] = (
        facts_ref[...].reshape(blocks, 8, LANES).astype(BF16)
    )


def match_kernel(
    recv_ref, images_ref, above_ref, below_ref,
    table_ref, forward_ref, form_ref, across_ref, out_ref,
    framed_ref, facts_ref, whole_ref, scalar_ref, list_ref, data_ref, cross_ref,
    energy_ref, tall_ref, wide_ref, copy_sem,
):
    blocks = recv_ref.shape[0]
    dates = images_ref.shape[0]
    half = CHIP // 2
    facts_ref[...] = recv_ref[:, 2 * CHIP : 2 * CHIP + 8, :].astype(F32).reshape(blocks * 8, LANES)
    whole = [facts_ref[pl.ds(rank, blocks, stride=8), :].astype(BF16) for rank in range(2)]
    if blocks < CHIP // 2:
        whole.append(jnp.zeros((CHIP - 2 * blocks, LANES), BF16))
    lane16 = lax.broadcasted_iota(jnp.int32, (16, LANES), 1)
    row16 = lax.broadcasted_iota(jnp.int32, (16, LANES), 0)
    choose = (lane16 == row16).astype(F32).astype(BF16)
    fact = dot_nt(choose, jnp.concatenate(whole + whole, axis=0))
    whole_ref[...] = fact[:8].astype(jnp.int32)
    copy = pltpu.make_async_copy(whole_ref, scalar_ref, copy_sem)
    copy.start()
    framed_ref[:, :SMAX, :] = above_ref[...].astype(F32)
    framed_ref[:, SMAX : SMAX + CHIP, :] = images_ref[...].astype(F32)
    framed_ref[:, SMAX + CHIP :, :] = below_ref[...].astype(F32)
    for ref in (energy_ref, tall_ref, wide_ref):
        ref[...] = jnp.zeros(ref.shape, F32)
    copy.wait()

    count = 0
    for slot in range(2 * blocks):
        list_ref[count] = slot
        count = count + scalar_ref[0, slot]
    spare = CHIP
    for extra in range(BATCH):
        list_ref[count + extra] = spare
    lane = lax.broadcasted_iota(jnp.int32, (1, LANES), 1)
    low = lane < CHIP
    level = level_lanes()
    turn_sign = jnp.where(lane % half == 0, 0.0, jnp.where(low, 1.0, -1.0))
    corner = jnp.where((lane % half == 0) & (lane >= CHIP), 1.0, 0.0)
    top_row = lax.broadcasted_iota(jnp.int32, (8, LANES), 0) == 0

    def one_batch(turn, carry):
        rows_of = []
        near_of = []
        for s in range(BATCH):
            slot = list_ref[turn * BATCH + s]
            rows_of.append(slot)
            source = jnp.where(slot == spare, 0, slot)
            rank = jnp.where(source >= blocks, 1, 0)
            near_of.append((source - rank * blocks, pl.multiple_of(rank * CHIP, CHIP)))
            second = scalar_ref[1, source]
            pieces = []
            starts = []
            for chip in range(2):
                down = scalar_ref[2 + 2 * chip, source] + SMAX
                start = scalar_ref[3 + 2 * chip, source]
                piece = framed_ref[second, pl.ds(down, CHIP), :]
                pieces.append(pltpu.roll(piece, lax.rem(LANES - start, LANES), 1))
                starts.append(start)
            column = lane + jnp.where(low, starts[0], starts[1])
            inside = (column >= 0) & (column < LANES)
            window = jnp.where(low, pieces[0], pieces[1])
            data_ref[s * CHIP : (s + 1) * CHIP, :] = jnp.where(inside, window, 0.0).astype(BF16)
        section = dot(data_ref[...], table_ref[...])
        crosses = []
        for s in range(BATCH):
            part = section[s * CHIP : (s + 1) * CHIP, :LANES]
            part = part - level * jnp.sum(part, axis=0, keepdims=True)
            other = section[s * CHIP : (s + 1) * CHIP, LANES:]
            far = dot(forward_ref[...], jnp.concatenate([part, other], axis=1).astype(BF16))
            block, at = near_of[s]
            near = recv_ref[block, pl.ds(at, CHIP), :].astype(F32)
            turned = pltpu.roll(near, CHIP, 1) * turn_sign
            top, low_rows = near[:half], near[half:]
            top_turned, low_turned = turned[:half], turned[half:]
            p, q = far[:half, :LANES], far[:half, LANES:]
            p_low, q_low = far[half:, :LANES], far[half:, LANES:]
            first = top * p + top_turned * q
            second = low_rows * p_low + low_turned * q_low
            upper = first + second
            lower = (low_rows * p + low_turned * q) - (top * p_low + top_turned * q_low)
            upper = jnp.concatenate([jnp.where(top_row, first[:8], upper[:8]), upper[8:]], axis=0)
            lower = jnp.concatenate([jnp.where(top_row, second[:8], lower[:8]), lower[8:]], axis=0)
            cross = jnp.concatenate([upper, lower], axis=0)
            crosses.append(cross)
            cross_ref[s * CHIP : (s + 1) * CHIP, :] = cross.astype(BF16)
        wide = dot(cross_ref[...], across_ref[...])
        for s in range(0, BATCH, 2):
            pair = [cross_ref[r * CHIP : (r + 1) * CHIP, :] for r in (s, s + 1)]
            tall = dot(form_ref[...], jnp.concatenate(pair, axis=1))
            for r in range(2):
                cross = crosses[s + r]
                power = cross * cross
                tall_r = cross * tall[:, r * LANES : (r + 1) * LANES]
                wide_r = cross * wide[(s + r) * CHIP : (s + r + 1) * CHIP]
                at = pl.ds(rows_of[s + r], 1)
                energy_ref[at, :] = 0.5 * (
                    jnp.sum(power, axis=0, keepdims=True)
                    + power[:1] + corner * power[half : half + 1]
                )
                tall_ref[at, :] = jnp.sum(tall_r, axis=0, keepdims=True)
                wide_ref[at, :] = 0.5 * (jnp.sum(wide_r, axis=0, keepdims=True) + wide_r[:1])
        return carry

    lax.fori_loop(0, (count + BATCH - 1) // BATCH, one_batch, 0)

    lane8 = lax.broadcasted_iota(jnp.int32, (8, LANES), 1)
    row8 = lax.broadcasted_iota(jnp.int32, (8, LANES), 0)
    weights = jnp.where((row8 == 1) | ((lane8 % half == 0) & (lane8 < CHIP)), 1.0, 0.5)
    even = lane // half % 2 == 0
    stack = []
    for ref in (energy_ref, tall_ref, wide_ref):
        value = ref[:CHIP, :]
        stack += [jnp.where(even, value, 0.0), jnp.where(even, 0.0, value)]
    weights = weights.astype(BF16)
    found = sum(dot_nt(weights, part) for part in parts_of(jnp.concatenate(stack, axis=0), 3))
    norm = found[0:1, :LANES] + 1e-6
    tall = found[0:1, LANES : 2 * LANES] / norm
    wide = found[1:2, 2 * LANES :] / norm
    live = fact[0:1] > 0.5
    down = jnp.where(live, jnp.where(low, fact[2:3], fact[4:5]) + tall, 0.0)
    across = jnp.where(live, jnp.where(low, fact[7:8], fact[8:9]) + wide, 0.0)
    row = lax.broadcasted_iota(jnp.int32, (LANES, LANES), 0)
    row = jnp.where(row < CHIP, -1, row % dates).astype(F32)
    chosen = (row == fact[1:2]).astype(F32).astype(BF16)
    value = jnp.where(row8 < 2, down, across)
    value = jnp.where((row8 < 4) & ((row8 % 2 == 0) == (lane8 < CHIP)), value, 0.0)
    sums = dot_nt(jnp.concatenate(parts_of(value, 3), axis=0), chosen)
    sums = sums[:8] + sums[8:16] + sums[16:24]
    sums = jnp.where((lane8 - CHIP) // dates == row8, sums, 0.0)
    sums = jnp.sum(sums, axis=0, keepdims=True)
    sums = jnp.where(low, fact[6:7], sums)
    result = jnp.where(row8 == 0, down, jnp.where(row8 == 1, across, sums))
    for block in range(blocks):
        out_ref[block] = result[:4]


def series_kernel(
    own_ref, result_ref, firsts_ref, seconds_ref, offsets_ref, series_ref
):
    blocks = result_ref.shape[0] // 4
    slots = own_ref.shape[0]
    dates = seconds_ref.shape[0]
    me = lax.axis_index("date").astype(F32)
    own = own_ref[...]
    partner = lax.broadcasted_iota(jnp.int32, (slots, blocks), 1).astype(F32)
    partner = (own[:, 0:1] == partner).astype(F32).astype(BF16)
    lane = lax.broadcasted_iota(jnp.int32, (slots, LANES), 1)
    mine = lane.astype(F32) - me == own[:, 1:2] + jnp.where(lane < CHIP, 0.0, float(CHIP))
    mine = mine & (own[:, 1:2] >= 0.0)
    facts = result_ref[pl.ds(2, blocks, stride=4), :]
    low = lax.broadcasted_iota(jnp.int32, (blocks, LANES), 1) < CHIP
    first = jnp.where(low, facts, pltpu.roll(facts, CHIP, 1))
    lane8 = lax.broadcasted_iota(jnp.int32, (8, LANES), 1)
    row8 = lax.broadcasted_iota(jnp.int32, (8, LANES), 0)
    chips = (lane8 // CHIP == row8).astype(F32).astype(BF16)
    pieces = ((lane8 - CHIP) // dates == row8).astype(F32).astype(BF16)
    total = jnp.concatenate(
        [jnp.sum(seconds_ref[date] * facts, axis=0, keepdims=True) for date in range(dates)],
        axis=0,
    )
    gained = sum(dot_nt(pieces, part) for part in parts_of(total, 3))
    for axis in range(2):
        rows = result_ref[pl.ds(axis, blocks, stride=4), :]
        value = sum(dot(partner, part) for part in parts_of(rows, 3))
        value = jnp.where(mine, value, 0.0)
        value = sum(dot_nt(chips, part) for part in parts_of(value, 3))
        offsets_ref[axis] = value[:2]
        total = jnp.zeros((dates, LANES), F32)
        for date in range(dates):
            here = jnp.sum(jnp.where(first == date, rows, 0.0), axis=0, keepdims=True)
            total = total + firsts_ref[axis, date] * here
        lost = sum(dot_nt(chips, part) for part in parts_of(total, 3))
        series_ref[axis] = gained[2 * axis : 2 * axis + 2] - lost[:2]


def body(images, inverse_blocks, pair_first, pair_block, pair_second, pair_count, shifts, anchors):
    blocks = lax.axis_size("date")
    strips = lax.axis_size("strip")
    dates, length, columns = images.shape
    slots = pair_first.shape[0]
    hbm = pl.BlockSpec(memory_space=pltpu.HBM)
    vmem = pl.BlockSpec(memory_space=pltpu.VMEM)
    params = pltpu.CompilerParams(vmem_limit_bytes=48 * 2**20)
    ends = strips - 1
    above = lax.ppermute(
        images[:, length - SMAX :, :], "strip", [(i, i + 1) for i in range(ends)]
    )
    below = lax.ppermute(images[:, :SMAX, :], "strip", [(i + 1, i) for i in range(ends)])
    turned = inverse_blocks.reshape(2, 2, dates, blocks, dates).transpose(0, 4, 2, 1, 3)
    turned = jnp.concatenate([turned, turned], axis=4)
    turned = jnp.pad(turned, ((0, 0),) * 4 + ((0, CHIP - 2 * blocks),))
    firsts = turned.reshape(2, dates, dates, LANES)
    seconds = inverse_blocks.reshape(2, 2, dates, blocks, dates).transpose(2, 3, 0, 1, 4)
    seconds = jnp.pad(seconds.reshape(dates, blocks, 4 * dates), ((0, 0), (0, 0), (CHIP, 0)))
    near_table, far_table, forward, form, across = [jnp.asarray(t) for t in make_tables()]
    send, own = pl.pallas_call(
        pack_kernel,
        out_shape=(
            jax.ShapeDtypeStruct((blocks, 2 * length + 8, columns), BF16),
            jax.ShapeDtypeStruct((slots, columns), F32),
        ),
        in_specs=[hbm] * 9,
        out_specs=(vmem, vmem),
        scratch_shapes=[
            pltpu.VMEM(images.shape, BF16),
            pltpu.VMEM(near_table.shape, BF16),
            pltpu.VMEM(forward.shape, BF16),
            pltpu.SMEM((slots,), jnp.int32),
            pltpu.SMEM((slots,), jnp.int32),
            pltpu.SMEM((slots,), jnp.int32),
            pltpu.SMEM((1,), jnp.int32),
            pltpu.SMEM((2, 2, slots), jnp.int32),
            pltpu.SMEM((2,), jnp.int32),
            pltpu.VMEM((dates, length, columns), BF16),
            pltpu.VMEM((blocks * 8, columns), F32),
            pltpu.SMEM((blocks,), jnp.int32),
            pltpu.SMEM((slots,), jnp.int32),
            pltpu.SemaphoreType.DMA((9,)),
        ],
        compiler_params=pltpu.CompilerParams(vmem_limit_bytes=60 * 2**20),
    )(
        pair_first, pair_block[:, 0], pair_second, pair_count,
        jnp.transpose(shifts, (1, 2, 0)), anchors, images, near_table, forward,
    )
    recv = lax.all_to_all(send, "date", split_axis=0, concat_axis=0, tiled=True)
    recv, firsts, seconds = lax.optimization_barrier((recv, firsts, seconds))
    result = pl.pallas_call(
        match_kernel,
        out_shape=jax.ShapeDtypeStruct((blocks, 4, columns), F32),
        in_specs=[vmem] * 8,
        out_specs=vmem,
        scratch_shapes=[
            pltpu.VMEM((dates, length + 2 * SMAX, columns), F32),
            pltpu.VMEM((blocks * 8, columns), F32),
            pltpu.VMEM((8, columns), jnp.int32),
            pltpu.SMEM((8, columns), jnp.int32),
            pltpu.SMEM((CHIP + BATCH,), jnp.int32),
            pltpu.VMEM((BATCH * length, columns), BF16),
            pltpu.VMEM((BATCH * length, columns), BF16),
            pltpu.VMEM((CHIP + 8, columns), F32),
            pltpu.VMEM((CHIP + 8, columns), F32),
            pltpu.VMEM((CHIP + 8, columns), F32),
            pltpu.SemaphoreType.DMA,
        ],
        compiler_params=params,
    )(recv, images, above, below, far_table, forward, form, across)
    result = lax.all_to_all(result, "date", split_axis=0, concat_axis=0, tiled=True)
    offsets, series = pl.pallas_call(
        series_kernel,
        out_shape=(
            jax.ShapeDtypeStruct((2, 2, slots), F32),
            jax.ShapeDtypeStruct((2, 2, dates), F32),
        ),
        in_specs=[vmem] * 4,
        out_specs=(vmem, vmem),
        compiler_params=params,
    )(own, result.reshape(blocks * 4, columns), firsts, seconds)
    return jnp.transpose(offsets, (2, 0, 1)), series


def solution(mesh):
    return jax.shard_map(
        body,
        mesh=mesh,
        in_specs=(
            P("date", "strip", None),
            P(None, "strip", "date", None),
            P("date"),
            P("date", None),
            P("date"),
            P("date"),
            P("date", None, "strip"),
            P("strip"),
        ),
        out_specs=(P("date", None, "strip"), P(None, "strip", "date")),
        check_vma=False,
    )
```
